256 devices in a mesh: ctx: 32 (over z, x), tp: 8 (over y, core).
Axes of the slice: x: 4, y: 4, z: 8, core: 2. Of those that a mesh axis runs over, the one named last changes fastest.
Arguments:
- lengths: int32 [32], replicated, may hold values from 1 to 288, 6144 in all
- queries: bfloat16 [9216, 8192], P('ctx', 'tp'), may hold values from -10 to 10
- keys: bfloat16 [9216, 1024], P('ctx', 'tp'), may hold values from -6 to 6
- values: bfloat16 [9216, 1024], P('ctx', 'tp'), may hold values from -8 to 8
- out_weight: bfloat16 [8192, 8192], P('tp', 'ctx'), may hold values from -0.125 to 0.125
Outputs:
- mixed: bfloat16 [9216, 8192], P('ctx', 'tp')
The draws below stay inside these ranges and needn't reach their ends.
All inputs are finite; a program needn't handle non-finite values.
Results may differ from the reference program's by a relative error of at most 0.019.
Values may be sent and summed in bfloat16 or wider, within the bound.
A program may use at most 64 MiB of HBM per device.

```python
import math
import jax
import jax.numpy as jnp
import numpy as np
from jax import lax

D = 8192
KVH = 8
HD = 128
HQ = 64
CAP = 288
TOTAL = 6144
ROWS = 9216
N_CTX = 32
N_TP = 8


def draw_keys(key, part):
    key = jax.random.fold_in(key, 11)
    base = jnp.clip(jax.random.normal(key, (ROWS, KVH, HD), jnp.float32), -6.0, 6.0)
    return base.reshape(ROWS, KVH * HD).astype(jnp.bfloat16)


def draw_queries(key, part):
    key = jax.random.fold_in(key, 23)
    group = HQ // KVH
    base = jnp.clip(2.5 * jax.random.normal(key, (ROWS, KVH, group, HD), jnp.float32), -10.0, 10.0)
    return base.reshape(ROWS, HQ * HD).astype(jnp.bfloat16)


def strengthened(result, key, source, target, parts, factor):
    owner, partner = [(jnp.arange(result.shape[axis_at]) // (result.shape[axis_at] // parts)).reshape([-1 if axis == axis_at else 1 for axis in range(result.ndim)]) for axis_at in (source, target)]
    chosen = jax.random.permutation(key, parts)[partner]
    strong = (owner == chosen) | (owner == (partner + parts // 2) % parts)
    return jnp.where(strong, factor * result, result)


def level_of(key, dims, cuts, low, high):
    factor_of = 1.0
    for dim, blocks in cuts:
        steps = jax.random.uniform(jax.random.fold_in(jax.random.fold_in(key, 6), dim), (blocks,), jnp.float32, low / len(cuts), high / len(cuts))
        factor_of = factor_of * jnp.repeat(jnp.exp(steps), dims[dim] // blocks).reshape((-1,) + (1,) * (len(dims) - 1 - dim))
    return factor_of


def length_profile(number_of, total, reach, slope):
    weights = [(1 << 20) // math.isqrt(standing ** slope) + 1 for standing in range(2, number_of + 1)]
    rest, holding = total - reach - (number_of - 1), [1] * (number_of - 1)
    while rest > 0:
        movable = [i for i in range(number_of - 1) if holding[i] < reach]
        whole, left = sum([weights[i] for i in movable]), rest
        for i in movable:
            extra = min(reach - holding[i], max(1, left * weights[i] // whole), rest)
            holding[i] = holding[i] + extra
            rest = rest - extra
    return np.array([reach] + holding)


def ragged(key, amount, total, bound, slope):
    if amount == 2:
        one = jax.random.randint(key, (), max(1, total - bound), min(bound, total - 1) + 1)
        return jnp.stack([one, total - one])
    sizes = jnp.asarray(length_profile(amount, total, bound, slope), jnp.int32)
    twos = (amount - 1) // 2
    giver, taker = sizes[1:1 + 2 * twos:2], sizes[2:2 + 2 * twos:2]
    slack = jnp.minimum(giver - 1, bound - taker)
    moved = jax.random.randint(jax.random.fold_in(key, 1), (twos,), 0, 1 << 20) % (slack + 1)
    sizes = sizes.at[1:1 + 2 * twos:2].set(giver - moved).at[2:2 + 2 * twos:2].set(taker + moved)
    return sizes[jax.random.permutation(jax.random.fold_in(key, 2), amount)]


def scatter_about(key, dims, scale, most, cuts=(), held_as=jnp.bfloat16):
    level = level_of(key, dims, cuts, -0.22, 0.18) if cuts else 1.0
    entries = jax.random.normal(key, dims, jnp.float32) * scale * level
    return jnp.minimum(jnp.maximum(entries, -most), most).astype(held_as)


def gaussian_with(rng, shape, scale, bound, cuts, heavy, kind=jnp.bfloat16):
    values = scale * jax.random.normal(rng, shape, jnp.float32)
    if cuts:
        values = values * level_of(rng, shape, cuts, -0.22, 0.18)
    return jnp.clip(strengthened(values, jax.random.fold_in(rng, 3), *heavy), -bound, bound).astype(kind)


def setup_inputs(seed: int = 0) -> dict:
    streams_of = jax.random.split(jax.random.key(seed), 6)
    return {
        "lengths": ragged(streams_of[0], N_CTX, TOTAL, CAP, 2).astype(jnp.int32),
        "queries": draw_queries(jax.random.fold_in(streams_of[5], 71), 0),
        "keys": draw_keys(jax.random.fold_in(streams_of[5], 71), 0),
        "values": scatter_about(streams_of[3], (ROWS, KVH * HD), 2.0, 8.0, ((0, 32), (1, 8))),
        "out_weight": gaussian_with(streams_of[4], (HQ * HD, D), (HQ * HD) ** -0.5, 0.125, ((0, 8), (1, 32)), (0, 1, 32, 2.75)),
    }


def reference(lengths, queries, keys, values, out_weight):
    group = HQ // KVH
    scale = HD ** -0.5
    starts = (jnp.cumsum(lengths) - lengths).astype(jnp.int32)
    slot_rows = jnp.arange(CAP, dtype=jnp.int32)
    position = (starts[:, None] + slot_rows[None, :]).reshape(-1)
    live = (slot_rows[None, :] < lengths[:, None]).reshape(-1)
    pieces = []
    for stretch in range(N_CTX):
        upper = (stretch + 1) * CAP
        quad = queries[stretch * CAP:upper].astype(jnp.float32).reshape(CAP, KVH, group, HD)
        key_all = keys[:upper].astype(jnp.float32).reshape(upper, KVH, HD)
        value_all = values[:upper].astype(jnp.float32).reshape(upper, KVH, HD)
        query_pos = position[stretch * CAP:upper]
        allowed = live[None, :upper] & (position[None, :upper] <= query_pos[:, None])

        def one_head(index):
            scores = jnp.einsum("rgd,sd->rgs", quad[:, index], key_all[:, index]) * scale
            scores = jnp.where(allowed[:, None, :], scores, -1e30)
            peak = jnp.max(scores, axis=-1, keepdims=True)
            weights = jnp.where(allowed[:, None, :], jnp.exp(scores - peak), 0.0)
            norm = jnp.sum(weights, axis=-1)
            rounded = lax.optimization_barrier(weights.astype(jnp.bfloat16))
            accum = jnp.einsum("rgs,sd->rgd", rounded.astype(jnp.float32), value_all[:, index])
            return accum / norm[..., None]

        heads = lax.map(one_head, jnp.arange(KVH, dtype=jnp.int32))
        pieces.append(jnp.transpose(heads, (1, 0, 2, 3)).reshape(CAP, HQ * HD))
    attn = jnp.concatenate(pieces, axis=0)
    attn = jnp.where(live[:, None], attn, 0.0).astype(jnp.bfloat16)
    width = HQ * HD // N_TP
    total = jnp.zeros((N_CTX * CAP, D), jnp.float32)
    for part_index in range(N_TP):
        lower = part_index * width
        partial_value = jnp.dot(attn[:, lower:lower + width], out_weight[lower:lower + width], preferred_element_type=jnp.float32).astype(jnp.bfloat16)
        partial_value = lax.optimization_barrier(partial_value)
        total = total + partial_value.astype(jnp.float32)
    return total.astype(jnp.bfloat16)
```

```python
import math

import jax
import jax.numpy as jnp
from jax import lax
from jax.experimental import pallas as pl
from jax.experimental.pallas import tpu as pltpu
from jax.sharding import PartitionSpec as P

HD = 128
NZ, NX, NY = 8, 4, 4
SLOTS = 288
HEADS = 8
KEYS = NX * SLOTS
HALF = SLOTS // 2
WIDE = 256
DEPTH = 1024
PIECE = DEPTH // 2
UNITS = 2 * NX
SCALE = math.log2(math.e) * HD**-0.5
MESH = pl.DeviceIdType.MESH


def ring(value, size):
    return lax.rem(value + size, size)


def chunk_offset(s):
    odd = lax.rem(s, 2)
    return lax.div(s, 2) * (1 - odd) - lax.div(s + 1, 2) * odd


def unit_place(u):
    g = lax.div(u + 2, 4)
    mid = lax.rem(g, 2)
    i = mid * (1 + lax.rem(u, 2)) + lax.div(g, 2) * 3
    r = mid * lax.div(u + 2 - 4 * mid, 2) + (1 - mid) * lax.rem(u, 2)
    return i, r


def x_offset(i):
    return i + lax.div(i, 2) - 2 * lax.div(i, 3)


def kernel(
    lengths, q, k, v, w, out,
    kv, live, acc, peak, wbuf, abuf, csend, crecv, own, rsend, rrecv, msend, mrecv, fbuf, obuf,
    local, zs, zr, xs1, xr1, xs2, xr2, ws, wr, as1, as2, ar, cs, cr, rs, rr, ms, mr, fs, fr,
):
    me_c = lax.axis_index("ctx")
    me_t = lax.axis_index("tp")
    z, x = lax.div(me_c, NX), lax.rem(me_c, NX)
    y, core = lax.div(me_t, 2), lax.rem(me_t, 2)

    def on_z(d):
        return (ring(z + d, NZ) * NX + x, me_t)

    def on_x(d):
        return (z * NX + ring(x + d, NX), me_t)

    def on_y(d):
        return (me_c, ring(y + d, NY) * 2 + core)

    z_up, z_down = on_z(1), on_z(-1)
    x_right, x_left = on_x(1), on_x(-1)
    y_up, y_down = on_y(1), on_y(-1)
    twin = (me_c, y * 2 + 1 - core)

    def remote(src, dst, send, recv, device):
        return pltpu.make_async_remote_copy(
            src_ref=src, dst_ref=dst, send_sem=send, recv_sem=recv,
            device_id=device, device_id_type=MESH,
        )

    barrier = pltpu.get_barrier_semaphore()
    for device in (z_up, z_down, x_right, x_left, on_x(2), y_up, y_down, twin):
        pl.semaphore_signal(barrier, inc=1, device_id=device, device_id_type=MESH)

    w_copy = pltpu.make_async_copy(w, wbuf.at[z], local.at[0])
    w_copy.start()

    def span(column):
        return pl.ds(pl.multiple_of(column * SLOTS, SLOTS), SLOTS)

    own_length = lengths[me_c]
    mine = span(x)
    alive = lax.broadcasted_iota(jnp.int32, (SLOTS, HD), 0) < own_length
    key = k[...].astype(jnp.float32)
    kv[z, 0, mine, :] = jnp.where(alive, key, key[0:1, :]).astype(jnp.bfloat16)
    kv[z, 1, mine, :] = jnp.where(alive, v[...].astype(jnp.float32), 0.0).astype(jnp.bfloat16)

    pl.semaphore_wait(barrier, 8)

    def z_block(zp):
        return kv.at[zp, :, mine, :]

    def z_both(zp, send, arrival, device):
        return remote(z_block(zp), z_block(zp), zs.at[send], zr.at[arrival], device)

    def z_one(zp, which, send, arrival, device):
        block = kv.at[zp, which, mine, :]
        return remote(block, block, zs.at[send], zr.at[arrival], device)

    def zp_of(s):
        return ring(z + chunk_offset(s), NZ)

    def z_forward(j, act):
        zp = zp_of(j)
        step = 2 * lax.rem(j, 2) - 1
        device = (ring(z + step, NZ) * NX + x, me_t)

        @pl.when(j <= 4)
        def _():
            act(z_both(zp, j, j + 2, device))

        @pl.when(j == 5)
        def _():
            act(z_one(zp, 0, j, 7, device))

        @pl.when(j == 6)
        def _():
            act(z_one(zp, 1, j, 8, device))

    def z_arrival(j):
        zp = zp_of(j)

        @pl.when(j <= 6)
        def _():
            z_both(zp, j, j, z_up).wait_recv()

        @pl.when(j == 7)
        def _():
            z_one(zp, 0, 0, 7, z_up).wait_recv()
            z_one(zp, 1, 0, 8, z_down).wait_recv()

    def x_first(j, way, column):
        zp = zp_of(j)
        block = kv.at[zp, :, span(column), :]
        return remote(block, block, xs1.at[way, j], xr1.at[way, j], (x_right, x_left)[way])

    def x_second(j, way, column):
        zp = zp_of(j)
        block = kv.at[zp, way, span(column), :]
        return remote(block, block, xs2.at[way, j], xr2.at[way, j], (x_right, x_left)[way])

    left, right, across = ring(x - 1, NX), ring(x + 1, NX), ring(x + 2, NX)

    def needed(j):
        return zp_of(j) <= z

    def x_start(j):
        @pl.when(needed(j))
        def _():
            x_first(j, 0, x).start()
            x_first(j, 1, x).start()

    def x_forward(j):
        @pl.when(needed(j))
        def _():
            x_first(j, 0, left).wait_recv()
            x_second(j, 0, left).start()
            x_first(j, 1, right).wait_recv()
            x_second(j, 1, right).start()

    def w_copy_of(i, way, held):
        hop = lax.div(i, 2) + held
        half = lax.rem(i, 2) if way == 0 else 1 - lax.rem(i, 2)
        block = ring(z - hop, NZ) if way == 0 else ring(z + hop, NZ)
        part = wbuf.at[block, pl.ds(pl.multiple_of(half * PIECE, PIECE), PIECE), :]
        return remote(part, part, ws.at[way, i], wr.at[way, i], (z_up, z_down)[way])

    def w_send(i):
        @pl.when(i >= 2)
        def _():
            w_copy_of(i - 2, 0, 1).wait_recv()
            w_copy_of(i - 2, 1, 1).wait_recv()

        w_copy_of(i, 0, 0).start()
        w_copy_of(i, 1, 0).start()

    z_both(z, 0, 1, z_up).start()
    z_both(z, 7, 2, z_down).start()
    x_first(0, 0, x).start()
    x_first(0, 1, x).start()
    w_copy.wait()
    w_send(0)
    w_send(1)

    rows_at = lax.broadcasted_iota(jnp.int32, (SLOTS, HD), 0)

    def mark(c, carry):
        block = (rows_at < lengths[c]).astype(jnp.float32).astype(jnp.bfloat16)
        live[lax.div(c, NX), span(lax.rem(c, NX)), :] = block
        return carry

    lax.fori_loop(0, NZ * NX, mark, 0)

    z_arrival(1)
    z_forward(1, lambda copy: copy.start())
    x_start(1)
    x_forward(0)

    def attend(zp, first):
        def head(h, carry):
            query = q[:, pl.ds(pl.multiple_of(h * HD, HD), HD)]
            s = lax.dot_general(
                query, kv[zp, 0], (((1,), (1,)), ((), ())), preferred_element_type=jnp.float32
            )
            if first:
                slot = x * SLOTS + lax.broadcasted_iota(jnp.int32, (SLOTS, KEYS), 0)
                at = lax.broadcasted_iota(jnp.int32, (SLOTS, KEYS), 1)
                s = jnp.where(at <= slot, s, -1e30)
            top = jnp.max(s, axis=1, keepdims=True)
            if not first:
                before = peak[h][:, 0:1]
                top = jnp.maximum(top, before)
            weights = jnp.exp2(s * SCALE - top * SCALE).astype(jnp.bfloat16)
            terms = jnp.concatenate([kv[zp, 1], live[zp]], axis=1)
            part = jnp.dot(weights, terms, preferred_element_type=jnp.float32)
            if first:
                acc[h] = part
            else:
                acc[h] = acc[h] * jnp.exp2((before - top) * SCALE) + part
            peak[h] = jnp.broadcast_to(top, (SLOTS, HD))
            return carry

        lax.fori_loop(0, HEADS, head, 0)

    def chunk(s, carry):
        @pl.when(s <= 5)
        def _():
            z_arrival(s + 2)
            z_forward(s + 2, lambda copy: copy.start())

        @pl.when(s <= 6)
        def _():
            x_forward(s + 1)

        @pl.when(s <= 5)
        def _():
            x_start(s + 2)

        @pl.when((s >= 2) & (s <= 6))
        def _():
            w_send(s)

        @pl.when(needed(s))
        def _():
            x_second(s, 0, across).wait_recv()
            x_second(s, 1, across).wait_recv()

        @pl.when(s == 0)
        def _():
            attend(z, True)

        @pl.when((s > 0) & needed(s))
        def _():
            attend(zp_of(s), False)

        return carry

    lax.fori_loop(0, NZ, chunk, 0)

    def a_first(r, way):
        block = abuf.at[x, r]
        return remote(block, block, as1.at[way, r], ar.at[2 - way, r], (x_right, x_left)[way])

    def a_second(way):
        block = abuf.at[(left, right)[way], way]
        return remote(block, block, as2.at[way], ar.at[3, way], (x_right, x_left)[way])

    def finish(r, carry):
        rows = pl.ds(pl.multiple_of(r * HALF, HALF), HALF)
        kept = lax.broadcasted_iota(jnp.int32, (HALF, HD), 0) + r * HALF < own_length

        def head(h, inner):
            a = acc[h, rows, :]
            o = jnp.where(kept, a[:, :HD] / a[:, HD:], 0.0).astype(jnp.bfloat16)
            abuf[x, r, :, pl.ds(pl.multiple_of(h * HD, HD), HD)] = o
            return inner

        lax.fori_loop(0, HEADS, head, 0)
        a_first(r, 0).start()
        a_first(r, 1).start()
        return carry

    lax.fori_loop(0, 2, finish, 0)
    for i in (5, 6):
        w_copy_of(i, 0, 1).wait_recv()
        w_copy_of(i, 1, 1).wait_recv()

    def twin_copy(u):
        return remote(csend.at[u], crecv.at[u], cs.at[u], cr.at[u], twin)

    def relay(u, way):
        return remote(
            rsend.at[u, way], rrecv.at[u, way], rs.at[u, way], rr.at[u, way], (y_up, y_down)[way]
        )

    def main(u, way):
        return remote(
            msend.at[u, way], mrecv.at[u, way], ms.at[u, way], mr.at[u, way], (y_up, y_down)[way]
        )

    def home(u, i, r):
        place = obuf.at[
            pl.ds(pl.multiple_of(r * HALF, HALF), HALF), pl.ds(pl.multiple_of(x * WIDE, WIDE), WIDE)
        ]
        seen = 3 - i + 3 * lax.div(i, 3)
        device = (z * NX + ring(x + x_offset(i), NX), me_t)
        return remote(fbuf.at[u], place, fs.at[u], fr.at[seen, r], device)

    def project(u):
        i, r = unit_place(u)
        column = ring(x + x_offset(i), NX)

        @pl.when(i > 0)
        def _():
            block = abuf.at[column, r]
            remote(block, block, as2.at[0], ar.at[i, r], x_right).wait_recv()

        @pl.when(u == 3)
        def _():
            a_second(0).start()

        @pl.when(u == 4)
        def _():
            a_second(1).start()

        def theirs(j, carry):
            csend[u, j] = jnp.dot(
                abuf[column, r], wbuf[j * 2 + 1 - core], preferred_element_type=jnp.float32
            ).astype(jnp.bfloat16)
            return carry

        lax.fori_loop(0, NY, theirs, 0)
        twin_copy(u).start()

        def ours(j, carry):
            own[u, j] = jnp.dot(
                abuf[column, r], wbuf[j * 2 + core], preferred_element_type=jnp.float32
            )
            return carry

        lax.fori_loop(0, NY, ours, 0)

    def both(u, j):
        return own[u, j] + crecv[u, j].astype(jnp.float32)

    def add_twin(u):
        twin_copy(u).wait_recv()
        total = both(u, ring(y + 2, NY)).astype(jnp.bfloat16)
        rsend[u, 0] = total[:, :HD]
        rsend[u, 1] = total[:, HD:]
        relay(u, 0).start()
        relay(u, 1).start()

    def add_relay(u):
        relay(u, 0).wait_recv()
        relay(u, 1).wait_recv()
        total = both(u, ring(y + 1, NY))
        msend[u, 0, :, :HD] = (total[:, :HD] + rrecv[u, 0].astype(jnp.float32)).astype(jnp.bfloat16)
        msend[u, 0, :, HD:] = total[:, HD:].astype(jnp.bfloat16)
        main(u, 0).start()
        total = both(u, ring(y - 1, NY))
        msend[u, 1, :, :HD] = total[:, :HD].astype(jnp.bfloat16)
        msend[u, 1, :, HD:] = (total[:, HD:] + rrecv[u, 1].astype(jnp.float32)).astype(jnp.bfloat16)
        main(u, 1).start()

    def add_main(u):
        main(u, 0).wait_recv()
        main(u, 1).wait_recv()
        total = both(u, y) + mrecv[u, 0].astype(jnp.float32) + mrecv[u, 1].astype(jnp.float32)
        total = total.astype(jnp.bfloat16)
        i, r = unit_place(u)

        @pl.when(i == 0)
        def _():
            obuf[
                pl.ds(pl.multiple_of(r * HALF, HALF), HALF),
                pl.ds(pl.multiple_of(x * WIDE, WIDE), WIDE),
            ] = total

        @pl.when(i > 0)
        def _():
            fbuf[u] = total
            home(u, i, r).start()

    def unit(n, carry):
        @pl.when((n >= 1) & (n <= UNITS))
        def _():
            add_twin(n - 1)

        @pl.when((n >= 2) & (n <= UNITS + 1))
        def _():
            add_relay(n - 2)

        @pl.when(n >= 3)
        def _():
            add_main(n - 3)

        @pl.when(n < UNITS)
        def _():
            project(n)

        return carry

    lax.fori_loop(0, UNITS + 3, unit, 0)

    def arrived(n, carry):
        i, r = 1 + lax.div(n, 2), lax.rem(n, 2)
        place = obuf.at[
            pl.ds(pl.multiple_of(r * HALF, HALF), HALF),
            pl.ds(pl.multiple_of(ring(x + x_offset(i), NX) * WIDE, WIDE), WIDE),
        ]
        remote(fbuf.at[0], place, fs.at[0], fr.at[i, r], x_right).wait_recv()
        return carry

    lax.fori_loop(0, UNITS - 2, arrived, 0)
    out_copy = pltpu.make_async_copy(obuf, out, local.at[0])
    out_copy.start()

    z_both(z, 0, 1, z_up).wait_send()
    z_both(z, 7, 2, z_down).wait_send()

    def sent_chunk(j, carry):
        @pl.when(j > 0)
        def _():
            z_forward(j, lambda copy: copy.wait_send())

        @pl.when(needed(j))
        def _():
            for way in (0, 1):
                x_first(j, way, x).wait_send()
                x_second(j, way, (left, right)[way]).wait_send()

        @pl.when(j <= 6)
        def _():
            w_copy_of(j, 0, 0).wait_send()
            w_copy_of(j, 1, 0).wait_send()

        return carry

    lax.fori_loop(0, NZ, sent_chunk, 0)
    for way in (0, 1):
        a_first(0, way).wait_send()
        a_first(1, way).wait_send()
        a_second(way).wait_send()

    def sent_unit(u, carry):
        twin_copy(u).wait_send()
        for way in (0, 1):
            relay(u, way).wait_send()
            main(u, way).wait_send()

        @pl.when(u >= 2)
        def _():
            i, r = unit_place(u)
            home(u, i, r).wait_send()

        return carry

    lax.fori_loop(0, UNITS, sent_unit, 0)
    out_copy.wait()


def shards(lengths, queries, keys, values, out_weight):
    bf16, f32 = jnp.bfloat16, jnp.float32
    dma = pltpu.SemaphoreType.DMA
    vmem = pl.BlockSpec(memory_space=pltpu.VMEM)
    return pl.pallas_call(
        kernel,
        out_shape=jax.ShapeDtypeStruct(queries.shape, bf16),
        in_specs=[
            pl.BlockSpec(memory_space=pltpu.SMEM), vmem, vmem, vmem, pl.BlockSpec(memory_space=pl.ANY)
        ],
        out_specs=pl.BlockSpec(memory_space=pl.ANY),
        scratch_shapes=[
            pltpu.VMEM((NZ, 2, KEYS, HD), bf16),
            pltpu.VMEM((NZ, KEYS, HD), bf16),
            pltpu.VMEM((HEADS, SLOTS, 2 * HD), f32),
            pltpu.VMEM((HEADS, SLOTS, HD), f32),
            pltpu.VMEM((NZ, DEPTH, WIDE), bf16),
            pltpu.VMEM((NX, 2, HALF, DEPTH), bf16),
            pltpu.VMEM((UNITS, NY, HALF, WIDE), bf16),
            pltpu.VMEM((UNITS, NY, HALF, WIDE), bf16),
            pltpu.VMEM((UNITS, NY, HALF, WIDE), f32),
            pltpu.VMEM((UNITS, 2, HALF, HD), bf16),
            pltpu.VMEM((UNITS, 2, HALF, HD), bf16),
            pltpu.VMEM((UNITS, 2, HALF, WIDE), bf16),
            pltpu.VMEM((UNITS, 2, HALF, WIDE), bf16),
            pltpu.VMEM((UNITS, HALF, WIDE), bf16),
            pltpu.VMEM((SLOTS, DEPTH), bf16),
            dma((1,)),
            dma((8,)), dma((9,)),
            dma((2, 8)), dma((2, 8)), dma((2, 8)), dma((2, 8)),
            dma((2, 7)), dma((2, 7)),
            dma((2, 2)), dma((2,)), dma((4, 2)),
            dma((UNITS,)), dma((UNITS,)),
            dma((UNITS, 2)), dma((UNITS, 2)),
            dma((UNITS, 2)), dma((UNITS, 2)),
            dma((UNITS,)), dma((4, 2)),
        ],
        compiler_params=pltpu.CompilerParams(
            collective_id=0, has_side_effects=True, vmem_limit_bytes=56 * 1024 * 1024
        ),
        cost_estimate=pl.CostEstimate(
            flops=16_000_000_000, bytes_accessed=4_000_000, transcendentals=21_000_000
        ),
    )(lengths, queries, keys, values, out_weight)


def solution(mesh):
    return jax.shard_map(
        shards,
        mesh=mesh,
        in_specs=(P(), P("ctx", "tp"), P("ctx", "tp"), P("ctx", "tp"), P("tp", "ctx")),
        out_specs=P("ctx", "tp"),
        check_vma=False,
    )
```

```python
import math

import jax
import jax.numpy as jnp
from jax import lax
from jax.experimental import pallas as pl
from jax.experimental.pallas import tpu as pltpu
from jax.sharding import PartitionSpec as P

HD = 128
NZ, NX, NY = 8, 4, 4
SLOTS = 288
HEADS = 8
KEYS = NX * SLOTS
HALF = SLOTS // 2
WIDE = 256
DEPTH = 1024
PARTS = 4
PIECE = DEPTH // PARTS
SENDS = 7 * PARTS // 2
UNITS = 2 * NX
SCALE = math.log2(math.e) * HD**-0.5
MESH = pl.DeviceIdType.MESH


def ring(value, size):
    return lax.rem(value + size, size)


def chunk_offset(s):
    odd = lax.rem(s, 2)
    return lax.div(s, 2) * (1 - odd) - lax.div(s + 1, 2) * odd


def unit_place(u):
    g = lax.div(u + 2, 4)
    mid = lax.rem(g, 2)
    i = mid * (1 + lax.rem(u, 2)) + lax.div(g, 2) * 3
    r = mid * lax.div(u + 2 - 4 * mid, 2) + (1 - mid) * lax.rem(u, 2)
    return i, r


def x_offset(i):
    return i + lax.div(i, 2) - 2 * lax.div(i, 3)


def kernel(
    lengths, q_in, k, v, w, out,
    q, kv, live, acc, peak, wbuf, abuf, csend, crecv, own, rsend, rrecv, msend, mrecv, fbuf, obuf,
    local, zs, zr, xs1, xr1, xs2, xr2, ws, wr, as1, as2, ar, cs, cr, rs, rr, ms, mr, fs, fr,
):
    me_c = lax.axis_index("ctx")
    me_t = lax.axis_index("tp")
    z, x = lax.div(me_c, NX), lax.rem(me_c, NX)
    y, core = lax.div(me_t, 2), lax.rem(me_t, 2)

    def on_z(d):
        return (ring(z + d, NZ) * NX + x, me_t)

    def on_x(d):
        return (z * NX + ring(x + d, NX), me_t)

    def on_y(d):
        return (me_c, ring(y + d, NY) * 2 + core)

    z_up, z_down = on_z(1), on_z(-1)
    x_right, x_left = on_x(1), on_x(-1)
    y_up, y_down = on_y(1), on_y(-1)
    twin = (me_c, y * 2 + 1 - core)

    def remote(src, dst, send, recv, device):
        return pltpu.make_async_remote_copy(
            src_ref=src, dst_ref=dst, send_sem=send, recv_sem=recv,
            device_id=device, device_id_type=MESH,
        )

    barrier = pltpu.get_barrier_semaphore()
    for device in (z_up, z_down, x_right, x_left, on_x(2), y_up, y_down, twin):
        pl.semaphore_signal(barrier, inc=1, device_id=device, device_id_type=MESH)

    w_copy = pltpu.make_async_copy(w, wbuf.at[z], local.at[0])
    w_copy.start()
    q_copy = pltpu.make_async_copy(q_in, q, local.at[1])
    q_copy.start()

    def span(column):
        return pl.ds(pl.multiple_of(column * SLOTS, SLOTS), SLOTS)

    own_length = lengths[me_c]
    mine = span(x)
    alive = lax.broadcasted_iota(jnp.int32, (SLOTS, HD), 0) < own_length
    key = k[...].astype(jnp.float32)
    kv[z, 0, mine, :] = jnp.where(alive, key, key[0:1, :]).astype(jnp.bfloat16)
    kv[z, 1, mine, :] = jnp.where(alive, v[...].astype(jnp.float32), 0.0).astype(jnp.bfloat16)

    pl.semaphore_wait(barrier, 8)

    def z_block(zp):
        return kv.at[zp, :, mine, :]

    def z_both(zp, send, arrival, device):
        return remote(z_block(zp), z_block(zp), zs.at[send], zr.at[arrival], device)

    def z_one(zp, which, send, arrival, device):
        block = kv.at[zp, which, mine, :]
        return remote(block, block, zs.at[send], zr.at[arrival], device)

    def zp_of(s):
        return ring(z + chunk_offset(s), NZ)

    def z_forward(j, act):
        zp = zp_of(j)
        step = 2 * lax.rem(j, 2) - 1
        device = (ring(z + step, NZ) * NX + x, me_t)

        @pl.when(j <= 4)
        def _():
            act(z_both(zp, j, j + 2, device))

        @pl.when(j == 5)
        def _():
            act(z_one(zp, 0, j, 7, device))

        @pl.when(j == 6)
        def _():
            act(z_one(zp, 1, j, 8, device))

    def z_arrival(j):
        zp = zp_of(j)

        @pl.when(j <= 6)
        def _():
            z_both(zp, j, j, z_up).wait_recv()

        @pl.when(j == 7)
        def _():
            z_one(zp, 0, 0, 7, z_up).wait_recv()
            z_one(zp, 1, 0, 8, z_down).wait_recv()

    def x_first(j, way, column):
        zp = zp_of(j)
        block = kv.at[zp, :, span(column), :]
        return remote(block, block, xs1.at[way, j], xr1.at[way, j], (x_right, x_left)[way])

    def x_second(j, way, column):
        zp = zp_of(j)
        block = kv.at[zp, way, span(column), :]
        return remote(block, block, xs2.at[way, j], xr2.at[way, j], (x_right, x_left)[way])

    left, right, across = ring(x - 1, NX), ring(x + 1, NX), ring(x + 2, NX)

    def needed(j):
        return zp_of(j) <= z

    def x_start(j):
        @pl.when(needed(j))
        def _():
            x_first(j, 0, x).start()
            x_first(j, 1, x).start()

    def x_forward(j):
        @pl.when(needed(j))
        def _():
            x_first(j, 0, left).wait_recv()
            x_second(j, 0, left).start()
            x_first(j, 1, right).wait_recv()
            x_second(j, 1, right).start()

    def w_copy_of(i, way, held):
        hop = lax.div(i, PARTS) + held
        turn = lax.rem(i, PARTS)
        at = turn if way == 0 else PARTS - 1 - turn
        block = ring(z - hop, NZ) if way == 0 else ring(z + hop, NZ)
        part = wbuf.at[block, pl.ds(pl.multiple_of(at * PIECE, PIECE), PIECE), :]
        return remote(part, part, ws.at[way, i], wr.at[way, i], (z_up, z_down)[way])

    def w_send(i):
        @pl.when(i >= PARTS)
        def _():
            w_copy_of(i - PARTS, 0, 1).wait_recv()
            w_copy_of(i - PARTS, 1, 1).wait_recv()

        w_copy_of(i, 0, 0).start()
        w_copy_of(i, 1, 0).start()

    def z_turn(j):
        z_arrival(j)
        z_forward(j, lambda copy: copy.start())

    z_both(z, 0, 1, z_up).start()
    z_both(z, 7, 2, z_down).start()
    x_start(0)
    w_copy.wait()
    w_send(0)

    rows_at = lax.broadcasted_iota(jnp.int32, (SLOTS, HD), 0)

    def mark(c, carry):
        block = (rows_at < lengths[c]).astype(jnp.float32).astype(jnp.bfloat16)
        live[lax.div(c, NX), span(lax.rem(c, NX)), :] = block
        return carry

    lax.fori_loop(0, NZ * NX, mark, 0)

    z_turn(1)
    z_turn(2)
    w_send(1)
    x_forward(0)
    x_start(1)
    x_start(2)
    z_turn(3)
    z_turn(4)
    w_send(2)
    x_forward(1)
    x_start(3)
    w_send(3)
    q_copy.wait()

    def attend(zp, first):
        def score(h):
            return lax.dot_general(
                q[:, h * HD:(h + 1) * HD], kv[zp, 0], (((1,), (1,)), ((), ())),
                preferred_element_type=jnp.float32,
            )

        if first:
            slot = x * SLOTS + lax.broadcasted_iota(jnp.int32, (SLOTS, KEYS), 0)
            blocked = lax.broadcasted_iota(jnp.int32, (SLOTS, KEYS), 1) > slot
        ahead = score(0)
        for h in range(HEADS):
            s = ahead
            if h + 1 < HEADS:
                ahead = score(h + 1)
            if first:
                s = jnp.where(blocked, -1e30, s)
            top = jnp.max(s, axis=1, keepdims=True)
            if not first:
                before = peak[h][:, 0:1]
                top = jnp.maximum(top, before)
            weights = jnp.exp2(s * SCALE - top * SCALE).astype(jnp.bfloat16)
            terms = jnp.concatenate([kv[zp, 1], live[zp]], axis=1)
            part = jnp.dot(weights, terms, preferred_element_type=jnp.float32)
            if first:
                acc[h] = part
            else:
                acc[h] = acc[h] * jnp.exp2((before - top) * SCALE) + part
            peak[h] = jnp.broadcast_to(top, (SLOTS, HD))

    def chunk(s, carry):
        @pl.when(s == 1)
        def _():
            z_turn(5)
            z_turn(6)

        @pl.when(s == 3)
        def _():
            z_turn(7)

        @pl.when(s <= 5)
        def _():
            x_forward(s + 2)

        @pl.when(s <= 3)
        def _():
            x_start(s + 4)

        @pl.when(s >= 1)
        def _():
            i = lax.div(3 * s + 5, 2)
            w_send(i)

            @pl.when(lax.rem(s, 2) == 0)
            def _():
                w_send(i + 1)

        @pl.when(needed(s))
        def _():
            x_second(s, 0, across).wait_recv()
            x_second(s, 1, across).wait_recv()

        @pl.when(s == 0)
        def _():
            attend(z, True)

        @pl.when((s > 0) & needed(s))
        def _():
            attend(zp_of(s), False)

        return carry

    lax.fori_loop(0, NZ, chunk, 0)

    def a_first(r, way):
        block = abuf.at[x, r]
        return remote(block, block, as1.at[way, r], ar.at[2 - way, r], (x_right, x_left)[way])

    def a_second(way):
        block = abuf.at[(left, right)[way], way]
        return remote(block, block, as2.at[way], ar.at[3, way], (x_right, x_left)[way])

    def finish(r, carry):
        rows = pl.ds(pl.multiple_of(r * HALF, HALF), HALF)
        kept = lax.broadcasted_iota(jnp.int32, (HALF, HD), 0) + r * HALF < own_length

        def head(h, inner):
            a = acc[h, rows, :]
            o = jnp.where(kept, a[:, :HD] / a[:, HD:], 0.0).astype(jnp.bfloat16)
            abuf[x, r, :, pl.ds(pl.multiple_of(h * HD, HD), HD)] = o
            return inner

        lax.fori_loop(0, HEADS, head, 0)
        a_first(r, 0).start()
        a_first(r, 1).start()
        return carry

    lax.fori_loop(0, 2, finish, 0)
    for i in range(SENDS - PARTS, SENDS):
        w_copy_of(i, 0, 1).wait_recv()
        w_copy_of(i, 1, 1).wait_recv()

    def twin_copy(u):
        return remote(csend.at[u], crecv.at[u], cs.at[u], cr.at[u], twin)

    def relay(u, way):
        return remote(
            rsend.at[u, way], rrecv.at[u, way], rs.at[u, way], rr.at[u, way], (y_up, y_down)[way]
        )

    def main(u, way):
        return remote(
            msend.at[u, way], mrecv.at[u, way], ms.at[u, way], mr.at[u, way], (y_up, y_down)[way]
        )

    def home(u, i, r):
        place = obuf.at[
            pl.ds(pl.multiple_of(r * HALF, HALF), HALF), pl.ds(pl.multiple_of(x * WIDE, WIDE), WIDE)
        ]
        seen = 3 - i + 3 * lax.div(i, 3)
        device = (z * NX + ring(x + x_offset(i), NX), me_t)
        return remote(fbuf.at[u], place, fs.at[u], fr.at[seen, r], device)

    def project(u):
        i, r = unit_place(u)
        column = ring(x + x_offset(i), NX)

        @pl.when(i > 0)
        def _():
            block = abuf.at[column, r]
            remote(block, block, as2.at[0], ar.at[i, r], x_right).wait_recv()

        @pl.when(u == 3)
        def _():
            a_second(0).start()

        @pl.when(u == 4)
        def _():
            a_second(1).start()

        rows = abuf[column, r]
        for j in range(NY):
            csend[u, j] = jnp.dot(
                rows, wbuf[j * 2 + 1 - core], preferred_element_type=jnp.float32
            ).astype(jnp.bfloat16)
        twin_copy(u).start()
        for j in range(NY):
            own[u, j] = jnp.dot(rows, wbuf[j * 2 + core], preferred_element_type=jnp.float32)

    def both(u, j):
        return own[u, j] + crecv[u, j].astype(jnp.float32)

    def add_twin(u):
        twin_copy(u).wait_recv()
        total = both(u, ring(y + 2, NY)).astype(jnp.bfloat16)
        rsend[u, 0] = total[:, :HD]
        rsend[u, 1] = total[:, HD:]
        relay(u, 0).start()
        relay(u, 1).start()

    def add_relay(u):
        relay(u, 0).wait_recv()
        relay(u, 1).wait_recv()
        total = both(u, ring(y + 1, NY))
        msend[u, 0, :, :HD] = (total[:, :HD] + rrecv[u, 0].astype(jnp.float32)).astype(jnp.bfloat16)
        msend[u, 0, :, HD:] = total[:, HD:].astype(jnp.bfloat16)
        main(u, 0).start()
        total = both(u, ring(y - 1, NY))
        msend[u, 1, :, :HD] = total[:, :HD].astype(jnp.bfloat16)
        msend[u, 1, :, HD:] = (total[:, HD:] + rrecv[u, 1].astype(jnp.float32)).astype(jnp.bfloat16)
        main(u, 1).start()

    def add_main(u):
        main(u, 0).wait_recv()
        main(u, 1).wait_recv()
        total = both(u, y) + mrecv[u, 0].astype(jnp.float32) + mrecv[u, 1].astype(jnp.float32)
        total = total.astype(jnp.bfloat16)
        i, r = unit_place(u)

        @pl.when(i == 0)
        def _():
            obuf[
                pl.ds(pl.multiple_of(r * HALF, HALF), HALF),
                pl.ds(pl.multiple_of(x * WIDE, WIDE), WIDE),
            ] = total

        @pl.when(i > 0)
        def _():
            fbuf[u] = total
            home(u, i, r).start()

    def group(g, carry):
        def project_one(u, inner):
            project(u)
            return inner

        def twin_one(u, inner):
            add_twin(u)
            return inner

        def relay_one(u, inner):
            add_relay(u)
            return inner

        lax.fori_loop(2 * g, 2 * g + 2, project_one, 0)
        lax.fori_loop(2 * g, 2 * g + 2, twin_one, 0)

        @pl.when(g > 0)
        def _():
            lax.fori_loop(2 * g - 2, 2 * g, main_one, 0)

        lax.fori_loop(2 * g, 2 * g + 2, relay_one, 0)
        return carry

    def main_one(u, carry):
        add_main(u)
        return carry

    lax.fori_loop(0, UNITS // 2, group, 0)
    lax.fori_loop(UNITS - 2, UNITS, main_one, 0)

    def arrived(n, carry):
        i, r = 1 + lax.div(n, 2), lax.rem(n, 2)
        place = obuf.at[
            pl.ds(pl.multiple_of(r * HALF, HALF), HALF),
            pl.ds(pl.multiple_of(ring(x + x_offset(i), NX) * WIDE, WIDE), WIDE),
        ]
        remote(fbuf.at[0], place, fs.at[0], fr.at[i, r], x_right).wait_recv()
        return carry

    lax.fori_loop(0, UNITS - 2, arrived, 0)
    out_copy = pltpu.make_async_copy(obuf, out, local.at[0])
    out_copy.start()

    z_both(z, 0, 1, z_up).wait_send()
    z_both(z, 7, 2, z_down).wait_send()

    def sent_chunk(j, carry):
        @pl.when(j > 0)
        def _():
            z_forward(j, lambda copy: copy.wait_send())

        @pl.when(needed(j))
        def _():
            for way in (0, 1):
                x_first(j, way, x).wait_send()
                x_second(j, way, (left, right)[way]).wait_send()

        return carry

    lax.fori_loop(0, NZ, sent_chunk, 0)

    def sent_piece(i, carry):
        w_copy_of(i, 0, 0).wait_send()
        w_copy_of(i, 1, 0).wait_send()
        return carry

    lax.fori_loop(0, SENDS, sent_piece, 0)
    for way in (0, 1):
        a_first(0, way).wait_send()
        a_first(1, way).wait_send()
        a_second(way).wait_send()

    def sent_unit(u, carry):
        twin_copy(u).wait_send()
        for way in (0, 1):
            relay(u, way).wait_send()
            main(u, way).wait_send()

        @pl.when(u >= 2)
        def _():
            i, r = unit_place(u)
            home(u, i, r).wait_send()

        return carry

    lax.fori_loop(0, UNITS, sent_unit, 0)
    out_copy.wait()


def shards(lengths, queries, keys, values, out_weight):
    bf16, f32 = jnp.bfloat16, jnp.float32
    dma = pltpu.SemaphoreType.DMA
    vmem = pl.BlockSpec(memory_space=pltpu.VMEM)
    any_space = pl.BlockSpec(memory_space=pl.ANY)
    return pl.pallas_call(
        kernel,
        out_shape=jax.ShapeDtypeStruct(queries.shape, bf16),
        in_specs=[
            pl.BlockSpec(memory_space=pltpu.SMEM), any_space, vmem, vmem, any_space
        ],
        out_specs=any_space,
        scratch_shapes=[
            pltpu.VMEM((SLOTS, DEPTH), bf16),
            pltpu.VMEM((NZ, 2, KEYS, HD), bf16),
            pltpu.VMEM((NZ, KEYS, HD), bf16),
            pltpu.VMEM((HEADS, SLOTS, 2 * HD), f32),
            pltpu.VMEM((HEADS, SLOTS, HD), f32),
            pltpu.VMEM((NZ, DEPTH, WIDE), bf16),
            pltpu.VMEM((NX, 2, HALF, DEPTH), bf16),
            pltpu.VMEM((UNITS, NY, HALF, WIDE), bf16),
            pltpu.VMEM((UNITS, NY, HALF, WIDE), bf16),
            pltpu.VMEM((UNITS, NY, HALF, WIDE), f32),
            pltpu.VMEM((UNITS, 2, HALF, HD), bf16),
            pltpu.VMEM((UNITS, 2, HALF, HD), bf16),
            pltpu.VMEM((UNITS, 2, HALF, WIDE), bf16),
            pltpu.VMEM((UNITS, 2, HALF, WIDE), bf16),
            pltpu.VMEM((UNITS, HALF, WIDE), bf16),
            pltpu.VMEM((SLOTS, DEPTH), bf16),
            dma((2,)),
            dma((8,)), dma((9,)),
            dma((2, 8)), dma((2, 8)), dma((2, 8)), dma((2, 8)),
            dma((2, SENDS)), dma((2, SENDS)),
            dma((2, 2)), dma((2,)), dma((4, 2)),
            dma((UNITS,)), dma((UNITS,)),
            dma((UNITS, 2)), dma((UNITS, 2)),
            dma((UNITS, 2)), dma((UNITS, 2)),
            dma((UNITS,)), dma((4, 2)),
        ],
        compiler_params=pltpu.CompilerParams(
            collective_id=0, has_side_effects=True, vmem_limit_bytes=56 * 1024 * 1024
        ),
        cost_estimate=pl.CostEstimate(
            flops=16_000_000_000, bytes_accessed=4_000_000, transcendentals=21_000_000
        ),
    )(lengths, queries, keys, values, out_weight)


def solution(mesh):
    return jax.shard_map(
        shards,
        mesh=mesh,
        in_specs=(P(), P("ctx", "tp"), P("ctx", "tp"), P("ctx", "tp"), P("tp", "ctx")),
        out_specs=P("ctx", "tp"),
        check_vma=False,
    )
```

```python
import math

import jax
import jax.numpy as jnp
from jax import lax
from jax.experimental import pallas as pl
from jax.experimental.pallas import tpu as pltpu
from jax.sharding import PartitionSpec as P

HD = 128
NZ, NX, NY = 8, 4, 4
SLOTS = 288
HEADS = 8
KEYS = NX * SLOTS
HALF = SLOTS // 2
WIDE = 256
DEPTH = 1024
PARTS = 4
PIECE = DEPTH // PARTS
SENDS = 7 * PARTS // 2
UNITS = 2 * NX
SCALE = math.log2(math.e) * HD**-0.5
MESH = pl.DeviceIdType.MESH


def ring(value, size):
    return lax.rem(value + size, size)


def chunk_offset(s):
    odd = lax.rem(s, 2)
    return lax.div(s, 2) * (1 - odd) - lax.div(s + 1, 2) * odd


def unit_place(u):
    g = lax.div(u + 2, 4)
    mid = lax.rem(g, 2)
    i = mid * (1 + lax.rem(u, 2)) + lax.div(g, 2) * 3
    r = mid * lax.div(u + 2 - 4 * mid, 2) + (1 - mid) * lax.rem(u, 2)
    return i, r


def x_offset(i):
    return i + lax.div(i, 2) - 2 * lax.div(i, 3)


def kernel(
    lengths, q_in, k, v, w, out,
    q, kv, live, acc, peak, wbuf, abuf, csend, crecv, own, rsend, rrecv, msend, mrecv, fbuf, obuf,
    local, zs, zr, xs1, xr1, xs2, xr2, ws, wr, as1, as2, ar, ar2, cs, cr, rs, rr, ms, mr, fs, fr,
):
    me_c = lax.axis_index("ctx")
    me_t = lax.axis_index("tp")
    z, x = lax.div(me_c, NX), lax.rem(me_c, NX)
    y, core = lax.div(me_t, 2), lax.rem(me_t, 2)

    def on_z(d):
        return (ring(z + d, NZ) * NX + x, me_t)

    def on_x(d):
        return (z * NX + ring(x + d, NX), me_t)

    def on_y(d):
        return (me_c, ring(y + d, NY) * 2 + core)

    z_up, z_down = on_z(1), on_z(-1)
    x_right, x_left = on_x(1), on_x(-1)
    y_up, y_down = on_y(1), on_y(-1)
    twin = (me_c, y * 2 + 1 - core)

    def remote(src, dst, send, recv, device):
        return pltpu.make_async_remote_copy(
            src_ref=src, dst_ref=dst, send_sem=send, recv_sem=recv,
            device_id=device, device_id_type=MESH,
        )

    barrier = pltpu.get_barrier_semaphore()
    for device in (z_up, z_down, x_right, x_left, on_x(2), y_up, y_down, twin):
        pl.semaphore_signal(barrier, inc=1, device_id=device, device_id_type=MESH)

    w_copy = pltpu.make_async_copy(w, wbuf.at[z], local.at[0])
    w_copy.start()
    q_copy = pltpu.make_async_copy(q_in, q, local.at[1])
    q_copy.start()

    def span(column):
        return pl.ds(pl.multiple_of(column * SLOTS, SLOTS), SLOTS)

    own_length = lengths[me_c]
    mine = span(x)
    alive = lax.broadcasted_iota(jnp.int32, (SLOTS, HD), 0) < own_length
    key = k[...].astype(jnp.float32)
    kv[z, 0, mine, :] = jnp.where(alive, key, key[0:1, :]).astype(jnp.bfloat16)
    kv[z, 1, mine, :] = jnp.where(alive, v[...].astype(jnp.float32), 0.0).astype(jnp.bfloat16)

    pl.semaphore_wait(barrier, 8)

    def z_block(zp):
        return kv.at[zp, :, mine, :]

    def z_both(zp, send, arrival, device):
        return remote(z_block(zp), z_block(zp), zs.at[send], zr.at[arrival], device)

    def z_one(zp, which, send, arrival, device):
        block = kv.at[zp, which, mine, :]
        return remote(block, block, zs.at[send], zr.at[arrival], device)

    def zp_of(s):
        return ring(z + chunk_offset(s), NZ)

    def z_forward(j, act):
        zp = zp_of(j)
        step = 2 * lax.rem(j, 2) - 1
        device = (ring(z + step, NZ) * NX + x, me_t)

        @pl.when(j <= 4)
        def _():
            act(z_both(zp, j, j + 2, device))

        @pl.when(j == 5)
        def _():
            act(z_one(zp, 0, j, 7, device))

        @pl.when(j == 6)
        def _():
            act(z_one(zp, 1, j, 8, device))

    def z_arrival(j):
        zp = zp_of(j)

        @pl.when(j <= 6)
        def _():
            z_both(zp, j, j, z_up).wait_recv()

        @pl.when(j == 7)
        def _():
            z_one(zp, 0, 0, 7, z_up).wait_recv()
            z_one(zp, 1, 0, 8, z_down).wait_recv()

    def x_first(j, way, column):
        zp = zp_of(j)
        block = kv.at[zp, :, span(column), :]
        return remote(block, block, xs1.at[way, j], xr1.at[way, j], (x_right, x_left)[way])

    def x_second(j, way, column):
        zp = zp_of(j)
        block = kv.at[zp, way, span(column), :]
        return remote(block, block, xs2.at[way, j], xr2.at[way, j], (x_right, x_left)[way])

    left, right, across = ring(x - 1, NX), ring(x + 1, NX), ring(x + 2, NX)

    def needed(j):
        return zp_of(j) <= z

    def x_start(j):
        @pl.when(needed(j))
        def _():
            x_first(j, 0, x).start()
            x_first(j, 1, x).start()

    def x_forward(j):
        @pl.when(needed(j))
        def _():
            x_first(j, 0, left).wait_recv()
            x_second(j, 0, left).start()
            x_first(j, 1, right).wait_recv()
            x_second(j, 1, right).start()

    def w_copy_of(i, way, held):
        hop = lax.div(i, PARTS) + held
        turn = lax.rem(i, PARTS)
        at = turn if way == 0 else PARTS - 1 - turn
        block = ring(z - hop, NZ) if way == 0 else ring(z + hop, NZ)
        part = wbuf.at[block, pl.ds(pl.multiple_of(at * PIECE, PIECE), PIECE), :]
        return remote(part, part, ws.at[way, i], wr.at[way, i], (z_up, z_down)[way])

    def w_send(i):
        @pl.when(i >= PARTS)
        def _():
            w_copy_of(i - PARTS, 0, 1).wait_recv()
            w_copy_of(i - PARTS, 1, 1).wait_recv()

        w_copy_of(i, 0, 0).start()
        w_copy_of(i, 1, 0).start()

    def z_turn(j):
        z_arrival(j)
        z_forward(j, lambda copy: copy.start())

    z_both(z, 0, 1, z_up).start()
    z_both(z, 7, 2, z_down).start()
    x_start(0)
    w_copy.wait()
    w_send(0)

    rows_at = lax.broadcasted_iota(jnp.int32, (SLOTS, HD), 0)

    def mark(c, carry):
        block = (rows_at < lengths[c]).astype(jnp.float32).astype(jnp.bfloat16)
        live[lax.div(c, NX), span(lax.rem(c, NX)), :] = block
        return carry

    lax.fori_loop(0, NZ * NX, mark, 0)

    z_turn(1)
    z_turn(2)
    w_send(1)
    x_forward(0)
    x_start(1)
    x_start(2)
    z_turn(3)
    z_turn(4)
    w_send(2)
    x_forward(1)
    x_start(3)
    w_send(3)
    q_copy.wait()

    def attend(zp, first, start, count):
        rows = slice(start, start + count)

        def score(h):
            return lax.dot_general(
                q[rows, h * HD:(h + 1) * HD], kv[zp, 0], (((1,), (1,)), ((), ())),
                preferred_element_type=jnp.float32,
            )

        if first:
            slot = x * SLOTS + start + lax.broadcasted_iota(jnp.int32, (count, KEYS), 0)
            blocked = lax.broadcasted_iota(jnp.int32, (count, KEYS), 1) > slot
        ahead = score(0)
        for h in range(HEADS):
            s = ahead
            if h + 1 < HEADS:
                ahead = score(h + 1)
            if first:
                s = jnp.where(blocked, -1e30, s)
            top = jnp.max(s, axis=1, keepdims=True)
            if not first:
                before = peak[h, rows, :][:, 0:1]
                top = jnp.maximum(top, before)
            weights = jnp.exp2(s * SCALE - top * SCALE).astype(jnp.bfloat16)
            terms = jnp.concatenate([kv[zp, 1], live[zp]], axis=1)
            part = jnp.dot(weights, terms, preferred_element_type=jnp.float32)
            if first:
                acc[h, rows, :] = part
            else:
                acc[h, rows, :] = acc[h, rows, :] * jnp.exp2((before - top) * SCALE) + part
            peak[h, rows, :] = jnp.broadcast_to(top, (count, HD))

    def chunk(s, carry):
        @pl.when(s == 1)
        def _():
            z_turn(5)
            z_turn(6)

        @pl.when(s == 3)
        def _():
            z_turn(7)

        @pl.when(s <= 3)
        def _():
            x_start(s + 4)

        @pl.when(s >= 1)
        def _():
            i = lax.div(3 * s + 5, 2)
            w_send(i)

            @pl.when(lax.rem(s, 2) == 0)
            def _():
                w_send(i + 1)

        @pl.when(needed(s))
        def _():
            x_second(s, 0, across).wait_recv()
            x_second(s, 1, across).wait_recv()

        @pl.when(s == 0)
        def _():
            attend(z, True, 0, SLOTS)

        @pl.when((s > 0) & (s < NZ - 1) & needed(s))
        def _():
            attend(zp_of(s), False, 0, SLOTS)

        @pl.when(s <= 5)
        def _():
            x_forward(s + 2)

        return carry

    lax.fori_loop(0, NZ, chunk, 0)

    def a_first(r, way):
        block = abuf.at[x, r]
        return remote(block, block, as1.at[way, r], ar.at[2 - way, r], (x_right, x_left)[way])

    def a_second(r, way):
        block = abuf.at[(left, right)[way], r, :, way * (DEPTH // 2):(way + 1) * (DEPTH // 2)]
        return remote(block, block, as2.at[way, r], ar2.at[way, r], (x_right, x_left)[way])

    for r in range(2):
        @pl.when(needed(NZ - 1))
        def _():
            attend(zp_of(NZ - 1), False, r * HALF, HALF)

        rows = slice(r * HALF, (r + 1) * HALF)
        kept = lax.broadcasted_iota(jnp.int32, (HALF, HD), 0) + r * HALF < own_length
        for h in range(HEADS):
            a = acc[h, rows, :]
            o = jnp.where(kept, a[:, :HD] / a[:, HD:], 0.0).astype(jnp.bfloat16)
            abuf[x, r, :, h * HD:(h + 1) * HD] = o
        a_first(r, 0).start()
        a_first(r, 1).start()

    for i in range(SENDS - PARTS, SENDS):
        w_copy_of(i, 0, 1).wait_recv()
        w_copy_of(i, 1, 1).wait_recv()

    def twin_copy(u):
        return remote(csend.at[u], crecv.at[u], cs.at[u], cr.at[u], twin)

    def relay(u, way):
        return remote(
            rsend.at[u, way], rrecv.at[u, way], rs.at[u, way], rr.at[u, way], (y_up, y_down)[way]
        )

    def main(u, way):
        return remote(
            msend.at[u, way], mrecv.at[u, way], ms.at[u, way], mr.at[u, way], (y_up, y_down)[way]
        )

    def home(u, i, r):
        place = obuf.at[
            pl.ds(pl.multiple_of(r * HALF, HALF), HALF), pl.ds(pl.multiple_of(x * WIDE, WIDE), WIDE)
        ]
        seen = 3 - i + 3 * lax.div(i, 3)
        device = (z * NX + ring(x + x_offset(i), NX), me_t)
        return remote(fbuf.at[u], place, fs.at[u], fr.at[seen, r], device)

    def project(u):
        i, r = unit_place(u)
        column = ring(x + x_offset(i), NX)

        @pl.when((i == 1) | (i == 2))
        def _():
            block = abuf.at[column, r]
            remote(block, block, as1.at[0, 0], ar.at[i, r], x_right).wait_recv()

        @pl.when(i == 2)
        def _():
            a_second(r, 0).start()

        @pl.when(i == 1)
        def _():
            a_second(r, 1).start()

        @pl.when(i == 3)
        def _():
            for way in (0, 1):
                block = abuf.at[across, r, :, way * (DEPTH // 2):(way + 1) * (DEPTH // 2)]
                remote(block, block, as2.at[way, r], ar2.at[way, r], x_right).wait_recv()

        rows = abuf[column, r]
        for j in range(NY):
            csend[u, j] = jnp.dot(
                rows, wbuf[j * 2 + 1 - core], preferred_element_type=jnp.float32
            ).astype(jnp.bfloat16)
        twin_copy(u).start()
        for j in range(NY):
            own[u, j] = jnp.dot(rows, wbuf[j * 2 + core], preferred_element_type=jnp.float32)

    def both(u, j):
        return own[u, j] + crecv[u, j].astype(jnp.float32)

    def add_twin(u):
        twin_copy(u).wait_recv()
        total = both(u, ring(y + 2, NY)).astype(jnp.bfloat16)
        rsend[u, 0] = total[:, :HD]
        rsend[u, 1] = total[:, HD:]
        relay(u, 0).start()
        relay(u, 1).start()

    def add_relay(u):
        relay(u, 0).wait_recv()
        relay(u, 1).wait_recv()
        total = both(u, ring(y + 1, NY))
        msend[u, 0, :, :HD] = (total[:, :HD] + rrecv[u, 0].astype(jnp.float32)).astype(jnp.bfloat16)
        msend[u, 0, :, HD:] = total[:, HD:].astype(jnp.bfloat16)
        main(u, 0).start()
        total = both(u, ring(y - 1, NY))
        msend[u, 1, :, :HD] = total[:, :HD].astype(jnp.bfloat16)
        msend[u, 1, :, HD:] = (total[:, HD:] + rrecv[u, 1].astype(jnp.float32)).astype(jnp.bfloat16)
        main(u, 1).start()

    def add_main(u):
        main(u, 0).wait_recv()
        main(u, 1).wait_recv()
        total = both(u, y) + mrecv[u, 0].astype(jnp.float32) + mrecv[u, 1].astype(jnp.float32)
        total = total.astype(jnp.bfloat16)
        i, r = unit_place(u)

        @pl.when(i == 0)
        def _():
            obuf[
                pl.ds(pl.multiple_of(r * HALF, HALF), HALF),
                pl.ds(pl.multiple_of(x * WIDE, WIDE), WIDE),
            ] = total

        @pl.when(i > 0)
        def _():
            fbuf[u] = total
            home(u, i, r).start()

    def sent_before():
        z_both(z, 0, 1, z_up).wait_send()
        z_both(z, 7, 2, z_down).wait_send()

        def sent_chunk(j, carry):
            @pl.when(j > 0)
            def _():
                z_forward(j, lambda copy: copy.wait_send())

            @pl.when(needed(j))
            def _():
                for way in (0, 1):
                    x_first(j, way, x).wait_send()
                    x_second(j, way, (left, right)[way]).wait_send()

            return carry

        lax.fori_loop(0, NZ, sent_chunk, 0)

        def sent_piece(i, carry):
            w_copy_of(i, 0, 0).wait_send()
            w_copy_of(i, 1, 0).wait_send()
            return carry

        lax.fori_loop(0, SENDS, sent_piece, 0)

    def unit(n, carry):
        @pl.when(n == 2)
        def _():
            sent_before()

        @pl.when((n >= 2) & (n < UNITS + 2))
        def _():
            add_relay(n - 2)

        @pl.when(n >= 4)
        def _():
            add_main(n - 4)

        @pl.when(n < UNITS)
        def _():
            project(n)
            add_twin(n)

        return carry

    lax.fori_loop(0, UNITS + 4, unit, 0)

    def arrived(n, carry):
        i, r = 1 + lax.div(n, 2), lax.rem(n, 2)
        place = obuf.at[
            pl.ds(pl.multiple_of(r * HALF, HALF), HALF),
            pl.ds(pl.multiple_of(ring(x + x_offset(i), NX) * WIDE, WIDE), WIDE),
        ]
        remote(fbuf.at[0], place, fs.at[0], fr.at[i, r], x_right).wait_recv()
        return carry

    lax.fori_loop(0, UNITS - 2, arrived, 0)
    out_copy = pltpu.make_async_copy(obuf, out, local.at[0])
    out_copy.start()

    for way in (0, 1):
        a_first(0, way).wait_send()
        a_first(1, way).wait_send()
        a_second(0, way).wait_send()
        a_second(1, way).wait_send()

    def sent_unit(u, carry):
        twin_copy(u).wait_send()
        for way in (0, 1):
            relay(u, way).wait_send()
            main(u, way).wait_send()

        @pl.when(u >= 2)
        def _():
            i, r = unit_place(u)
            home(u, i, r).wait_send()

        return carry

    lax.fori_loop(0, UNITS, sent_unit, 0)
    out_copy.wait()


def shards(lengths, queries, keys, values, out_weight):
    bf16, f32 = jnp.bfloat16, jnp.float32
    dma = pltpu.SemaphoreType.DMA
    vmem = pl.BlockSpec(memory_space=pltpu.VMEM)
    any_space = pl.BlockSpec(memory_space=pl.ANY)
    return pl.pallas_call(
        kernel,
        out_shape=jax.ShapeDtypeStruct(queries.shape, bf16),
        in_specs=[
            pl.BlockSpec(memory_space=pltpu.SMEM), any_space, vmem, vmem, any_space
        ],
        out_specs=any_space,
        scratch_shapes=[
            pltpu.VMEM((SLOTS, DEPTH), bf16),
            pltpu.VMEM((NZ, 2, KEYS, HD), bf16),
            pltpu.VMEM((NZ, KEYS, HD), bf16),
            pltpu.VMEM((HEADS, SLOTS, 2 * HD), f32),
            pltpu.VMEM((HEADS, SLOTS, HD), f32),
            pltpu.VMEM((NZ, DEPTH, WIDE), bf16),
            pltpu.VMEM((NX, 2, HALF, DEPTH), bf16),
            pltpu.VMEM((UNITS, NY, HALF, WIDE), bf16),
            pltpu.VMEM((UNITS, NY, HALF, WIDE), bf16),
            pltpu.VMEM((UNITS, NY, HALF, WIDE), f32),
            pltpu.VMEM((UNITS, 2, HALF, HD), bf16),
            pltpu.VMEM((UNITS, 2, HALF, HD), bf16),
            pltpu.VMEM((UNITS, 2, HALF, WIDE), bf16),
            pltpu.VMEM((UNITS, 2, HALF, WIDE), bf16),
            pltpu.VMEM((UNITS, HALF, WIDE), bf16),
            pltpu.VMEM((SLOTS, DEPTH), bf16),
            dma((2,)),
            dma((8,)), dma((9,)),
            dma((2, 8)), dma((2, 8)), dma((2, 8)), dma((2, 8)),
            dma((2, SENDS)), dma((2, SENDS)),
            dma((2, 2)), dma((2, 2)), dma((4, 2)), dma((2, 2)),
            dma((UNITS,)), dma((UNITS,)),
            dma((UNITS, 2)), dma((UNITS, 2)),
            dma((UNITS, 2)), dma((UNITS, 2)),
            dma((UNITS,)), dma((4, 2)),
        ],
        compiler_params=pltpu.CompilerParams(
            collective_id=0, has_side_effects=True, vmem_limit_bytes=56 * 1024 * 1024
        ),
        cost_estimate=pl.CostEstimate(
            flops=16_000_000_000, bytes_accessed=4_000_000, transcendentals=21_000_000
        ),
    )(lengths, queries, keys, values, out_weight)


def solution(mesh):
    return jax.shard_map(
        shards,
        mesh=mesh,
        in_specs=(P(), P("ctx", "tp"), P("ctx", "tp"), P("ctx", "tp"), P("tp", "ctx")),
        out_specs=P("ctx", "tp"),
        check_vma=False,
    )
```

```python
import math

import jax
import jax.numpy as jnp
from jax import lax
from jax.experimental import pallas as pl
from jax.experimental.pallas import tpu as pltpu
from jax.sharding import PartitionSpec as P

HD = 128
NZ, NX, NY = 8, 4, 4
SLOTS = 288
HEADS = 8
KEYS = NX * SLOTS
HALF = SLOTS // 2
WIDE = 256
DEPTH = 1024
PARTS = 4
PIECE = DEPTH // PARTS
SENDS = 7 * PARTS // 2
UNITS = 2 * NX
SCALE = math.log2(math.e) * HD**-0.5
MESH = pl.DeviceIdType.MESH


def ring(value, size):
    return lax.rem(value + size, size)


def chunk_offset(s):
    odd = lax.rem(s, 2)
    return lax.div(s, 2) * (1 - odd) - lax.div(s + 1, 2) * odd


def unit_place(u):
    g = lax.div(u + 2, 4)
    mid = lax.rem(g, 2)
    i = mid * (1 + lax.rem(u, 2)) + lax.div(g, 2) * 3
    r = mid * lax.div(u + 2 - 4 * mid, 2) + (1 - mid) * lax.rem(u, 2)
    return i, r


def x_offset(i):
    return i + lax.div(i, 2) - 2 * lax.div(i, 3)


def kernel(
    lengths, q_in, k, v, w, out,
    q, kv, live, acc, peak, wbuf, abuf, csend, crecv, own, rsend, rrecv, msend, mrecv, fbuf, obuf,
    local, zs, zr, xs1, xr1, xs2, xr2, ws, wr, as1, as2, ar, ar2, cs, cr, rs, rr, ms, mr, fs, fr,
):
    me_c = lax.axis_index("ctx")
    me_t = lax.axis_index("tp")
    z, x = lax.div(me_c, NX), lax.rem(me_c, NX)
    y, core = lax.div(me_t, 2), lax.rem(me_t, 2)

    def on_z(d):
        return (ring(z + d, NZ) * NX + x, me_t)

    def on_x(d):
        return (z * NX + ring(x + d, NX), me_t)

    def on_y(d):
        return (me_c, ring(y + d, NY) * 2 + core)

    z_up, z_down = on_z(1), on_z(-1)
    x_right, x_left = on_x(1), on_x(-1)
    y_up, y_down = on_y(1), on_y(-1)
    twin = (me_c, y * 2 + 1 - core)

    def remote(src, dst, send, recv, device):
        return pltpu.make_async_remote_copy(
            src_ref=src, dst_ref=dst, send_sem=send, recv_sem=recv,
            device_id=device, device_id_type=MESH,
        )

    barrier = pltpu.get_barrier_semaphore()
    for device in (z_up, z_down, x_right, x_left, on_x(2), y_up, y_down, twin):
        pl.semaphore_signal(barrier, inc=1, device_id=device, device_id_type=MESH)

    w_copy = pltpu.make_async_copy(w, wbuf.at[z], local.at[0])
    w_copy.start()
    q_copy = pltpu.make_async_copy(q_in, q, local.at[1])
    q_copy.start()

    def span(column):
        return pl.ds(pl.multiple_of(column * SLOTS, SLOTS), SLOTS)

    own_length = lengths[me_c]
    mine = span(x)
    alive = lax.broadcasted_iota(jnp.int32, (SLOTS, HD), 0) < own_length
    key = k[...].astype(jnp.float32)
    kv[z, 0, mine, :] = jnp.where(alive, key, key[0:1, :]).astype(jnp.bfloat16)
    kv[z, 1, mine, :] = jnp.where(alive, v[...].astype(jnp.float32), 0.0).astype(jnp.bfloat16)

    pl.semaphore_wait(barrier, 8)

    def z_block(zp):
        return kv.at[zp, :, mine, :]

    def z_both(zp, send, arrival, device):
        return remote(z_block(zp), z_block(zp), zs.at[send], zr.at[arrival], device)

    def z_one(zp, which, send, arrival, device):
        block = kv.at[zp, which, mine, :]
        return remote(block, block, zs.at[send], zr.at[arrival], device)

    def zp_of(s):
        return ring(z + chunk_offset(s), NZ)

    def z_forward(j, act):
        zp = zp_of(j)
        step = 2 * lax.rem(j, 2) - 1
        device = (ring(z + step, NZ) * NX + x, me_t)

        @pl.when(j <= 4)
        def _():
            act(z_both(zp, j, j + 2, device))

        @pl.when(j == 5)
        def _():
            act(z_one(zp, 0, j, 7, device))

        @pl.when(j == 6)
        def _():
            act(z_one(zp, 1, j, 8, device))

    def z_arrival(j):
        zp = zp_of(j)

        @pl.when(j <= 6)
        def _():
            z_both(zp, j, j, z_up).wait_recv()

        @pl.when(j == 7)
        def _():
            z_one(zp, 0, 0, 7, z_up).wait_recv()
            z_one(zp, 1, 0, 8, z_down).wait_recv()

    def x_first(j, way, column):
        zp = zp_of(j)
        block = kv.at[zp, :, span(column), :]
        return remote(block, block, xs1.at[way, j], xr1.at[way, j], (x_right, x_left)[way])

    def x_second(j, way, column):
        zp = zp_of(j)
        block = kv.at[zp, way, span(column), :]
        return remote(block, block, xs2.at[way, j], xr2.at[way, j], (x_right, x_left)[way])

    left, right, across = ring(x - 1, NX), ring(x + 1, NX), ring(x + 2, NX)

    def needed(j):
        return zp_of(j) <= z

    def x_start(j):
        @pl.when(needed(j))
        def _():
            x_first(j, 0, x).start()
            x_first(j, 1, x).start()

    def x_forward(j):
        @pl.when(needed(j))
        def _():
            x_first(j, 0, left).wait_recv()
            x_second(j, 0, left).start()
            x_first(j, 1, right).wait_recv()
            x_second(j, 1, right).start()

    def w_copy_of(i, way, held):
        hop = lax.div(i, PARTS) + held
        turn = lax.rem(i, PARTS)
        at = turn if way == 0 else PARTS - 1 - turn
        block = ring(z - hop, NZ) if way == 0 else ring(z + hop, NZ)
        part = wbuf.at[block, pl.ds(pl.multiple_of(at * PIECE, PIECE), PIECE), :]
        return remote(part, part, ws.at[way, i], wr.at[way, i], (z_up, z_down)[way])

    def w_send(i):
        @pl.when(i >= PARTS)
        def _():
            w_copy_of(i - PARTS, 0, 1).wait_recv()
            w_copy_of(i - PARTS, 1, 1).wait_recv()

        w_copy_of(i, 0, 0).start()
        w_copy_of(i, 1, 0).start()

    def z_turn(j):
        z_arrival(j)
        z_forward(j, lambda copy: copy.start())

    z_both(z, 0, 1, z_up).start()
    z_both(z, 7, 2, z_down).start()
    x_start(0)
    w_copy.wait()
    w_send(0)

    rows_at = lax.broadcasted_iota(jnp.int32, (SLOTS, HD), 0)

    def mark(c, carry):
        block = (rows_at < lengths[c]).astype(jnp.float32).astype(jnp.bfloat16)
        live[lax.div(c, NX), span(lax.rem(c, NX)), :] = block
        return carry

    lax.fori_loop(0, NZ * NX, mark, 0)

    z_turn(1)
    z_turn(2)
    w_send(1)
    x_forward(0)
    x_start(1)
    x_start(2)
    z_turn(3)
    z_turn(4)
    w_send(2)
    x_forward(1)
    x_start(3)
    w_send(3)
    q_copy.wait()

    def attend(zp, first, start, count):
        rows = slice(start, start + count)

        def score(h):
            return lax.dot_general(
                q[rows, h * HD:(h + 1) * HD], kv[zp, 0], (((1,), (1,)), ((), ())),
                preferred_element_type=jnp.float32,
            )

        if first:
            slot = x * SLOTS + start + lax.broadcasted_iota(jnp.int32, (count, KEYS), 0)
            blocked = lax.broadcasted_iota(jnp.int32, (count, KEYS), 1) > slot
        ahead = score(0)
        for h in range(HEADS):
            s = ahead
            if h + 1 < HEADS:
                ahead = score(h + 1)
            if first:
                s = jnp.where(blocked, -1e30, s)
            top = jnp.max(s, axis=1, keepdims=True)
            if not first:
                before = peak[h, rows, :][:, 0:1]
                top = jnp.maximum(top, before)
            weights = jnp.exp2(s * SCALE - top * SCALE).astype(jnp.bfloat16)
            terms = jnp.concatenate([kv[zp, 1], live[zp]], axis=1)
            part = jnp.dot(weights, terms, preferred_element_type=jnp.float32)
            if first:
                acc[h, rows, :] = part
            else:
                acc[h, rows, :] = acc[h, rows, :] * jnp.exp2((before - top) * SCALE) + part
            peak[h, rows, :] = jnp.broadcast_to(top, (count, HD))

    def chunk(s, carry):
        @pl.when(s == 1)
        def _():
            z_turn(5)
            z_turn(6)

        @pl.when(s == 3)
        def _():
            z_turn(7)

        @pl.when(s <= 3)
        def _():
            x_start(s + 4)

        @pl.when(s >= 1)
        def _():
            i = lax.div(3 * s + 5, 2)
            w_send(i)

            @pl.when(lax.rem(s, 2) == 0)
            def _():
                w_send(i + 1)

        @pl.when((s < NZ - 2) & needed(s))
        def _():
            x_second(s, 0, across).wait_recv()
            x_second(s, 1, across).wait_recv()

        @pl.when(s == 0)
        def _():
            attend(z, True, 0, SLOTS)

        @pl.when((s > 0) & (s < NZ - 2) & needed(s))
        def _():
            attend(zp_of(s), False, 0, SLOTS)

        @pl.when(s <= 5)
        def _():
            x_forward(s + 2)

        return carry

    lax.fori_loop(0, NZ, chunk, 0)

    def a_first(r, way):
        block = abuf.at[x, r]
        return remote(block, block, as1.at[way, r], ar.at[2 - way, r], (x_right, x_left)[way])

    def a_second(r, way):
        block = abuf.at[(left, right)[way], r, :, way * (DEPTH // 2):(way + 1) * (DEPTH // 2)]
        return remote(block, block, as2.at[way, r], ar2.at[way, r], (x_right, x_left)[way])

    for r in range(2):
        def last(s, carry):
            @pl.when(needed(s))
            def _():
                if r == 0:
                    x_second(s, 0, across).wait_recv()
                    x_second(s, 1, across).wait_recv()
                attend(zp_of(s), False, r * HALF, HALF)

            return carry

        lax.fori_loop(NZ - 2, NZ, last, 0)
        rows = slice(r * HALF, (r + 1) * HALF)
        kept = lax.broadcasted_iota(jnp.int32, (HALF, HD), 0) + r * HALF < own_length
        for h in range(HEADS):
            a = acc[h, rows, :]
            o = jnp.where(kept, a[:, :HD] / a[:, HD:], 0.0).astype(jnp.bfloat16)
            abuf[x, r, :, h * HD:(h + 1) * HD] = o
        a_first(r, 0).start()
        a_first(r, 1).start()

    for i in range(SENDS - PARTS, SENDS):
        w_copy_of(i, 0, 1).wait_recv()
        w_copy_of(i, 1, 1).wait_recv()

    def twin_copy(u):
        return remote(csend.at[u], crecv.at[u], cs.at[u], cr.at[u], twin)

    def relay(u, way):
        return remote(
            rsend.at[u, way], rrecv.at[u, way], rs.at[u, way], rr.at[u, way], (y_up, y_down)[way]
        )

    def main(u, way):
        return remote(
            msend.at[u, way], mrecv.at[u, way], ms.at[u, way], mr.at[u, way], (y_up, y_down)[way]
        )

    def home(u, i, r):
        place = obuf.at[
            pl.ds(pl.multiple_of(r * HALF, HALF), HALF), pl.ds(pl.multiple_of(x * WIDE, WIDE), WIDE)
        ]
        seen = 3 - i + 3 * lax.div(i, 3)
        device = (z * NX + ring(x + x_offset(i), NX), me_t)
        return remote(fbuf.at[u], place, fs.at[u], fr.at[seen, r], device)

    def project(u):
        i, r = unit_place(u)
        column = ring(x + x_offset(i), NX)

        @pl.when((i == 1) | (i == 2))
        def _():
            block = abuf.at[column, r]
            remote(block, block, as1.at[0, 0], ar.at[i, r], x_right).wait_recv()

        @pl.when(i == 2)
        def _():
            a_second(r, 0).start()

        @pl.when(i == 1)
        def _():
            a_second(r, 1).start()

        @pl.when(i == 3)
        def _():
            for way in (0, 1):
                block = abuf.at[across, r, :, way * (DEPTH // 2):(way + 1) * (DEPTH // 2)]
                remote(block, block, as2.at[way, r], ar2.at[way, r], x_right).wait_recv()

        rows = abuf[column, r]
        for j in range(NY):
            csend[u, j] = jnp.dot(
                rows, wbuf[j * 2 + 1 - core], preferred_element_type=jnp.float32
            ).astype(jnp.bfloat16)
        twin_copy(u).start()
        for j in range(NY):
            own[u, j] = jnp.dot(rows, wbuf[j * 2 + core], preferred_element_type=jnp.float32)

    def both(u, j):
        return own[u, j] + crecv[u, j].astype(jnp.float32)

    def add_twin(u):
        twin_copy(u).wait_recv()
        total = both(u, ring(y + 2, NY)).astype(jnp.bfloat16)
        rsend[u, 0] = total[:, :HD]
        rsend[u, 1] = total[:, HD:]
        relay(u, 0).start()
        relay(u, 1).start()

    def add_relay(u):
        relay(u, 0).wait_recv()
        relay(u, 1).wait_recv()
        total = both(u, ring(y + 1, NY))
        msend[u, 0, :, :HD] = (total[:, :HD] + rrecv[u, 0].astype(jnp.float32)).astype(jnp.bfloat16)
        msend[u, 0, :, HD:] = total[:, HD:].astype(jnp.bfloat16)
        main(u, 0).start()
        total = both(u, ring(y - 1, NY))
        msend[u, 1, :, :HD] = total[:, :HD].astype(jnp.bfloat16)
        msend[u, 1, :, HD:] = (total[:, HD:] + rrecv[u, 1].astype(jnp.float32)).astype(jnp.bfloat16)
        main(u, 1).start()

    def add_main(u):
        main(u, 0).wait_recv()
        main(u, 1).wait_recv()
        total = both(u, y) + mrecv[u, 0].astype(jnp.float32) + mrecv[u, 1].astype(jnp.float32)
        total = total.astype(jnp.bfloat16)
        i, r = unit_place(u)

        @pl.when(i == 0)
        def _():
            obuf[
                pl.ds(pl.multiple_of(r * HALF, HALF), HALF),
                pl.ds(pl.multiple_of(x * WIDE, WIDE), WIDE),
            ] = total

        @pl.when(i > 0)
        def _():
            fbuf[u] = total
            home(u, i, r).start()

    def sent_before():
        z_both(z, 0, 1, z_up).wait_send()
        z_both(z, 7, 2, z_down).wait_send()

        def sent_chunk(j, carry):
            @pl.when(j > 0)
            def _():
                z_forward(j, lambda copy: copy.wait_send())

            @pl.when(needed(j))
            def _():
                for way in (0, 1):
                    x_first(j, way, x).wait_send()
                    x_second(j, way, (left, right)[way]).wait_send()

            return carry

        lax.fori_loop(0, NZ, sent_chunk, 0)

        def sent_piece(i, carry):
            w_copy_of(i, 0, 0).wait_send()
            w_copy_of(i, 1, 0).wait_send()
            return carry

        lax.fori_loop(0, SENDS, sent_piece, 0)

    def unit(n, carry):
        @pl.when(n == 2)
        def _():
            sent_before()

        @pl.when((n >= 3) & (n < UNITS + 3))
        def _():
            add_relay(n - 3)

        @pl.when(n >= 6)
        def _():
            add_main(n - 6)

        @pl.when(n < UNITS)
        def _():
            project(n)

        @pl.when((n < UNITS - 2) & (lax.rem(n, 2) == 1))
        def _():
            add_twin(n - 1)
            add_twin(n)

        @pl.when((n >= UNITS - 2) & (n < UNITS))
        def _():
            add_twin(n)

        return carry

    lax.fori_loop(0, UNITS + 6, unit, 0)

    def arrived(n, carry):
        i, r = 1 + lax.div(n, 2), lax.rem(n, 2)
        place = obuf.at[
            pl.ds(pl.multiple_of(r * HALF, HALF), HALF),
            pl.ds(pl.multiple_of(ring(x + x_offset(i), NX) * WIDE, WIDE), WIDE),
        ]
        remote(fbuf.at[0], place, fs.at[0], fr.at[i, r], x_right).wait_recv()
        return carry

    lax.fori_loop(0, UNITS - 2, arrived, 0)
    out_copy = pltpu.make_async_copy(obuf, out, local.at[0])
    out_copy.start()

    for way in (0, 1):
        a_first(0, way).wait_send()
        a_first(1, way).wait_send()
        a_second(0, way).wait_send()
        a_second(1, way).wait_send()

    def sent_unit(u, carry):
        twin_copy(u).wait_send()
        for way in (0, 1):
            relay(u, way).wait_send()
            main(u, way).wait_send()

        @pl.when(u >= 2)
        def _():
            i, r = unit_place(u)
            home(u, i, r).wait_send()

        return carry

    lax.fori_loop(0, UNITS, sent_unit, 0)
    out_copy.wait()


def shards(lengths, queries, keys, values, out_weight):
    bf16, f32 = jnp.bfloat16, jnp.float32
    dma = pltpu.SemaphoreType.DMA
    vmem = pl.BlockSpec(memory_space=pltpu.VMEM)
    any_space = pl.BlockSpec(memory_space=pl.ANY)
    return pl.pallas_call(
        kernel,
        out_shape=jax.ShapeDtypeStruct(queries.shape, bf16),
        in_specs=[
            pl.BlockSpec(memory_space=pltpu.SMEM), any_space, vmem, vmem, any_space
        ],
        out_specs=any_space,
        scratch_shapes=[
            pltpu.VMEM((SLOTS, DEPTH), bf16),
            pltpu.VMEM((NZ, 2, KEYS, HD), bf16),
            pltpu.VMEM((NZ, KEYS, HD), bf16),
            pltpu.VMEM((HEADS, SLOTS, 2 * HD), f32),
            pltpu.VMEM((HEADS, SLOTS, HD), f32),
            pltpu.VMEM((NZ, DEPTH, WIDE), bf16),
            pltpu.VMEM((NX, 2, HALF, DEPTH), bf16),
            pltpu.VMEM((UNITS, NY, HALF, WIDE), bf16),
            pltpu.VMEM((UNITS, NY, HALF, WIDE), bf16),
            pltpu.VMEM((UNITS, NY, HALF, WIDE), f32),
            pltpu.VMEM((UNITS, 2, HALF, HD), bf16),
            pltpu.VMEM((UNITS, 2, HALF, HD), bf16),
            pltpu.VMEM((UNITS, 2, HALF, WIDE), bf16),
            pltpu.VMEM((UNITS, 2, HALF, WIDE), bf16),
            pltpu.VMEM((UNITS, HALF, WIDE), bf16),
            pltpu.VMEM((SLOTS, DEPTH), bf16),
            dma((2,)),
            dma((8,)), dma((9,)),
            dma((2, 8)), dma((2, 8)), dma((2, 8)), dma((2, 8)),
            dma((2, SENDS)), dma((2, SENDS)),
            dma((2, 2)), dma((2, 2)), dma((4, 2)), dma((2, 2)),
            dma((UNITS,)), dma((UNITS,)),
            dma((UNITS, 2)), dma((UNITS, 2)),
            dma((UNITS, 2)), dma((UNITS, 2)),
            dma((UNITS,)), dma((4, 2)),
        ],
        compiler_params=pltpu.CompilerParams(
            collective_id=0, has_side_effects=True, vmem_limit_bytes=56 * 1024 * 1024
        ),
        cost_estimate=pl.CostEstimate(
            flops=16_000_000_000, bytes_accessed=4_000_000, transcendentals=21_000_000
        ),
    )(lengths, queries, keys, values, out_weight)


def solution(mesh):
    return jax.shard_map(
        shards,
        mesh=mesh,
        in_specs=(P(), P("ctx", "tp"), P("ctx", "tp"), P("ctx", "tp"), P("tp", "ctx")),
        out_specs=P("ctx", "tp"),
        check_vma=False,
    )
```

```python
import math

import jax
import jax.numpy as jnp
from jax import lax
from jax.experimental import pallas as pl
from jax.experimental.pallas import tpu as pltpu
from jax.sharding import PartitionSpec as P

HD = 128
NZ, NX, NY = 8, 4, 4
SLOTS = 288
HEADS = 8
KEYS = NX * SLOTS
HALF = SLOTS // 2
WIDE = 256
DEPTH = 1024
PARTS = 4
PIECE = DEPTH // PARTS
SENDS = 7 * PARTS // 2
UNITS = 2 * NX
SCALE = math.log2(math.e) * HD**-0.5
MESH = pl.DeviceIdType.MESH


def ring(value, size):
    return lax.rem(value + size, size)


def chunk_offset(s):
    odd = lax.rem(s, 2)
    return lax.div(s, 2) * (1 - odd) - lax.div(s + 1, 2) * odd


def unit_place(u):
    g = lax.div(u + 2, 4)
    mid = lax.rem(g, 2)
    i = mid * (1 + lax.rem(u, 2)) + lax.div(g, 2) * 3
    r = mid * lax.div(u + 2 - 4 * mid, 2) + (1 - mid) * lax.rem(u, 2)
    return i, r


def x_offset(i):
    return i + lax.div(i, 2) - 2 * lax.div(i, 3)


def kernel(
    lengths, q_in, k, v, w, out,
    q, kv, live, acc, peak, wbuf, abuf, csend, crecv, own, rsend, rrecv, msend, mrecv, fbuf, obuf,
    local, zs, zr, xs1, xr1, xs2, xr2, ws, wr, as1, as2, ar, ar2, cs, cr, rs, rr, ms, mr, fs, fr,
):
    me_c = lax.axis_index("ctx")
    me_t = lax.axis_index("tp")
    z, x = lax.div(me_c, NX), lax.rem(me_c, NX)
    y, core = lax.div(me_t, 2), lax.rem(me_t, 2)

    def on_z(d):
        return (ring(z + d, NZ) * NX + x, me_t)

    def on_x(d):
        return (z * NX + ring(x + d, NX), me_t)

    def on_y(d):
        return (me_c, ring(y + d, NY) * 2 + core)

    z_up, z_down = on_z(1), on_z(-1)
    x_right, x_left = on_x(1), on_x(-1)
    y_up, y_down = on_y(1), on_y(-1)
    twin = (me_c, y * 2 + 1 - core)

    def remote(src, dst, send, recv, device):
        return pltpu.make_async_remote_copy(
            src_ref=src, dst_ref=dst, send_sem=send, recv_sem=recv,
            device_id=device, device_id_type=MESH,
        )

    barrier = pltpu.get_barrier_semaphore()
    for device in (z_up, z_down, x_right, x_left, on_x(2), y_up, y_down, twin):
        pl.semaphore_signal(barrier, inc=1, device_id=device, device_id_type=MESH)

    w_copy = pltpu.make_async_copy(w, wbuf.at[z], local.at[0])
    w_copy.start()
    q_copy = pltpu.make_async_copy(q_in, q, local.at[1])
    q_copy.start()

    def span(column):
        return pl.ds(pl.multiple_of(column * SLOTS, SLOTS), SLOTS)

    own_length = lengths[me_c]
    mine = span(x)
    alive = lax.broadcasted_iota(jnp.int32, (SLOTS, HD), 0) < own_length
    key = k[...].astype(jnp.float32)
    kv[z, 0, mine, :] = jnp.where(alive, key, key[0:1, :]).astype(jnp.bfloat16)
    kv[z, 1, mine, :] = jnp.where(alive, v[...].astype(jnp.float32), 0.0).astype(jnp.bfloat16)

    pl.semaphore_wait(barrier, 8)

    def z_block(zp):
        return kv.at[zp, :, mine, :]

    def z_both(zp, send, arrival, device):
        return remote(z_block(zp), z_block(zp), zs.at[send], zr.at[arrival], device)

    def z_one(zp, which, send, arrival, device):
        block = kv.at[zp, which, mine, :]
        return remote(block, block, zs.at[send], zr.at[arrival], device)

    def zp_of(s):
        return ring(z + chunk_offset(s), NZ)

    def z_forward(j, act):
        zp = zp_of(j)
        step = 2 * lax.rem(j, 2) - 1
        device = (ring(z + step, NZ) * NX + x, me_t)

        @pl.when(j <= 4)
        def _():
            act(z_both(zp, j, j + 2, device))

        @pl.when(j == 5)
        def _():
            act(z_one(zp, 0, j, 7, device))

        @pl.when(j == 6)
        def _():
            act(z_one(zp, 1, j, 8, device))

    def z_arrival(j):
        zp = zp_of(j)

        @pl.when(j <= 6)
        def _():
            z_both(zp, j, j, z_up).wait_recv()

        @pl.when(j == 7)
        def _():
            z_one(zp, 0, 0, 7, z_up).wait_recv()
            z_one(zp, 1, 0, 8, z_down).wait_recv()

    def x_first(j, way, column):
        zp = zp_of(j)
        block = kv.at[zp, :, span(column), :]
        return remote(block, block, xs1.at[way, j], xr1.at[way, j], (x_right, x_left)[way])

    def x_second(j, way, column):
        zp = zp_of(j)
        block = kv.at[zp, way, span(column), :]
        return remote(block, block, xs2.at[way, j], xr2.at[way, j], (x_right, x_left)[way])

    left, right, across = ring(x - 1, NX), ring(x + 1, NX), ring(x + 2, NX)

    def needed(j):
        return zp_of(j) <= z

    def x_start(j):
        @pl.when(needed(j))
        def _():
            x_first(j, 0, x).start()
            x_first(j, 1, x).start()

    def x_forward(j):
        @pl.when(needed(j))
        def _():
            x_first(j, 0, left).wait_recv()
            x_second(j, 0, left).start()
            x_first(j, 1, right).wait_recv()
            x_second(j, 1, right).start()

    def w_copy_of(i, way, held):
        hop = lax.div(i, PARTS) + held
        turn = lax.rem(i, PARTS)
        at = turn if way == 0 else PARTS - 1 - turn
        block = ring(z - hop, NZ) if way == 0 else ring(z + hop, NZ)
        part = wbuf.at[block, pl.ds(pl.multiple_of(at * PIECE, PIECE), PIECE), :]
        return remote(part, part, ws.at[way, i], wr.at[way, i], (z_up, z_down)[way])

    def w_send(i):
        @pl.when(i >= PARTS)
        def _():
            w_copy_of(i - PARTS, 0, 1).wait_recv()
            w_copy_of(i - PARTS, 1, 1).wait_recv()

        w_copy_of(i, 0, 0).start()
        w_copy_of(i, 1, 0).start()

    def z_turn(j):
        z_arrival(j)
        z_forward(j, lambda copy: copy.start())

    z_both(z, 0, 1, z_up).start()
    z_both(z, 7, 2, z_down).start()
    x_start(0)
    w_copy.wait()
    w_send(0)

    rows_at = lax.broadcasted_iota(jnp.int32, (SLOTS, HD), 0)

    def mark(c, carry):
        block = (rows_at < lengths[c]).astype(jnp.float32).astype(jnp.bfloat16)
        live[lax.div(c, NX), span(lax.rem(c, NX)), :] = block
        return carry

    lax.fori_loop(0, NZ * NX, mark, 0)

    z_turn(1)
    z_turn(2)
    w_send(1)
    x_forward(0)
    x_start(1)
    x_start(2)
    z_turn(3)
    z_turn(4)
    w_send(2)
    x_forward(1)
    x_start(3)
    w_send(3)
    q_copy.wait()

    def attend(zp, first, start, count):
        rows = slice(start, start + count)

        def score(h):
            return lax.dot_general(
                q[rows, h * HD:(h + 1) * HD], kv[zp, 0], (((1,), (1,)), ((), ())),
                preferred_element_type=jnp.float32,
            )

        if first:
            slot = x * SLOTS + start + lax.broadcasted_iota(jnp.int32, (count, KEYS), 0)
            blocked = lax.broadcasted_iota(jnp.int32, (count, KEYS), 1) > slot
        ahead = score(0)
        for h in range(HEADS):
            s = ahead
            if h + 1 < HEADS:
                ahead = score(h + 1)
            if first:
                s = jnp.where(blocked, -1e30, s)
            top = jnp.max(s, axis=1, keepdims=True)
            if not first:
                before = peak[h, rows, :][:, 0:1]
                top = jnp.maximum(top, before)
            weights = jnp.exp2(s * SCALE - top * SCALE).astype(jnp.bfloat16)
            terms = jnp.concatenate([kv[zp, 1], live[zp]], axis=1)
            part = jnp.dot(weights, terms, preferred_element_type=jnp.float32)
            if first:
                acc[h, rows, :] = part
            else:
                acc[h, rows, :] = acc[h, rows, :] * jnp.exp2((before - top) * SCALE) + part
            peak[h, rows, :] = jnp.broadcast_to(top, (count, HD))

    def chunk(s, carry):
        @pl.when(s == 1)
        def _():
            z_turn(5)
            z_turn(6)

        @pl.when(s == 3)
        def _():
            z_turn(7)

        @pl.when(s <= 3)
        def _():
            x_start(s + 4)

        @pl.when(s >= 1)
        def _():
            i = lax.div(3 * s + 5, 2)
            w_send(i)

            @pl.when(lax.rem(s, 2) == 0)
            def _():
                w_send(i + 1)

        @pl.when((s < NZ - 2) & needed(s))
        def _():
            x_second(s, 0, across).wait_recv()
            x_second(s, 1, across).wait_recv()

        @pl.when(s == 0)
        def _():
            attend(z, True, 0, SLOTS)

        @pl.when((s > 0) & (s < NZ - 2) & needed(s))
        def _():
            attend(zp_of(s), False, 0, SLOTS)

        @pl.when(s <= 5)
        def _():
            x_forward(s + 2)

        return carry

    lax.fori_loop(0, NZ, chunk, 0)

    def a_first(r, way):
        block = abuf.at[x, r]
        return remote(block, block, as1.at[way, r], ar.at[2 - way, r], (x_right, x_left)[way])

    def a_second(r, way):
        block = abuf.at[(left, right)[way], r, :, way * (DEPTH // 2):(way + 1) * (DEPTH // 2)]
        return remote(block, block, as2.at[way, r], ar2.at[way, r], (x_right, x_left)[way])

    for r in range(2):
        def last(s, carry):
            @pl.when(needed(s))
            def _():
                if r == 0:
                    x_second(s, 0, across).wait_recv()
                    x_second(s, 1, across).wait_recv()
                attend(zp_of(s), False, r * HALF, HALF)

            return carry

        lax.fori_loop(NZ - 2, NZ, last, 0)
        rows = slice(r * HALF, (r + 1) * HALF)
        kept = lax.broadcasted_iota(jnp.int32, (HALF, HD), 0) + r * HALF < own_length
        for h in range(HEADS):
            a = acc[h, rows, :]
            o = jnp.where(kept, a[:, :HD] / a[:, HD:], 0.0).astype(jnp.bfloat16)
            abuf[x, r, :, h * HD:(h + 1) * HD] = o
        a_first(r, 0).start()
        a_first(r, 1).start()

    early = z < NZ - 2

    def a_pass(r, way):
        block = abuf.at[(left, right)[way], r]
        remote(block, block, as1.at[way, r], ar.at[2 - way, r], x_right).wait_recv()
        a_second(r, way).start()

    @pl.when(early)
    def _():
        for r in range(2):
            a_pass(r, 0)
            a_pass(r, 1)

    for i in range(SENDS - PARTS, SENDS):
        w_copy_of(i, 0, 1).wait_recv()
        w_copy_of(i, 1, 1).wait_recv()

    def twin_copy(u):
        return remote(csend.at[u], crecv.at[u], cs.at[u], cr.at[u], twin)

    def relay(u, way):
        return remote(
            rsend.at[u, way], rrecv.at[u, way], rs.at[u, way], rr.at[u, way], (y_up, y_down)[way]
        )

    def main(u, way):
        return remote(
            msend.at[u, way], mrecv.at[u, way], ms.at[u, way], mr.at[u, way], (y_up, y_down)[way]
        )

    def home(u, i, r):
        place = obuf.at[
            pl.ds(pl.multiple_of(r * HALF, HALF), HALF), pl.ds(pl.multiple_of(x * WIDE, WIDE), WIDE)
        ]
        seen = 3 - i + 3 * lax.div(i, 3)
        device = (z * NX + ring(x + x_offset(i), NX), me_t)
        return remote(fbuf.at[u], place, fs.at[u], fr.at[seen, r], device)

    def project(u):
        i, r = unit_place(u)
        column = ring(x + x_offset(i), NX)

        @pl.when((i == 2) & (z >= NZ - 2))
        def _():
            a_pass(r, 0)

        @pl.when((i == 1) & (z >= NZ - 2))
        def _():
            a_pass(r, 1)

        @pl.when(i == 3)
        def _():
            for way in (0, 1):
                block = abuf.at[across, r, :, way * (DEPTH // 2):(way + 1) * (DEPTH // 2)]
                remote(block, block, as2.at[way, r], ar2.at[way, r], x_right).wait_recv()

        rows = abuf[column, r]
        for j in range(NY):
            csend[u, j] = jnp.dot(
                rows, wbuf[j * 2 + 1 - core], preferred_element_type=jnp.float32
            ).astype(jnp.bfloat16)
        twin_copy(u).start()
        for j in range(NY):
            own[u, j] = jnp.dot(rows, wbuf[j * 2 + core], preferred_element_type=jnp.float32)

    def both(u, j):
        return own[u, j] + crecv[u, j].astype(jnp.float32)

    def add_twin(u):
        twin_copy(u).wait_recv()
        total = both(u, ring(y + 2, NY)).astype(jnp.bfloat16)
        rsend[u, 0] = total[:, :HD]
        rsend[u, 1] = total[:, HD:]
        relay(u, 0).start()
        relay(u, 1).start()

    def add_relay(u):
        relay(u, 0).wait_recv()
        relay(u, 1).wait_recv()
        total = both(u, ring(y + 1, NY))
        msend[u, 0, :, :HD] = (total[:, :HD] + rrecv[u, 0].astype(jnp.float32)).astype(jnp.bfloat16)
        msend[u, 0, :, HD:] = total[:, HD:].astype(jnp.bfloat16)
        main(u, 0).start()
        total = both(u, ring(y - 1, NY))
        msend[u, 1, :, :HD] = total[:, :HD].astype(jnp.bfloat16)
        msend[u, 1, :, HD:] = (total[:, HD:] + rrecv[u, 1].astype(jnp.float32)).astype(jnp.bfloat16)
        main(u, 1).start()

    def add_main(u):
        main(u, 0).wait_recv()
        main(u, 1).wait_recv()
        total = both(u, y) + mrecv[u, 0].astype(jnp.float32) + mrecv[u, 1].astype(jnp.float32)
        total = total.astype(jnp.bfloat16)
        i, r = unit_place(u)

        @pl.when(i == 0)
        def _():
            obuf[
                pl.ds(pl.multiple_of(r * HALF, HALF), HALF),
                pl.ds(pl.multiple_of(x * WIDE, WIDE), WIDE),
            ] = total

        @pl.when(i > 0)
        def _():
            fbuf[u] = total
            home(u, i, r).start()

    def sent_before():
        z_both(z, 0, 1, z_up).wait_send()
        z_both(z, 7, 2, z_down).wait_send()

        def sent_chunk(j, carry):
            @pl.when(j > 0)
            def _():
                z_forward(j, lambda copy: copy.wait_send())

            @pl.when(needed(j))
            def _():
                for way in (0, 1):
                    x_first(j, way, x).wait_send()
                    x_second(j, way, (left, right)[way]).wait_send()

            return carry

        lax.fori_loop(0, NZ, sent_chunk, 0)

        def sent_piece(i, carry):
            w_copy_of(i, 0, 0).wait_send()
            w_copy_of(i, 1, 0).wait_send()
            return carry

        lax.fori_loop(0, SENDS, sent_piece, 0)

    def unit(n, carry):
        @pl.when(n == 2)
        def _():
            sent_before()

        @pl.when((n >= 3) & (n < UNITS + 3))
        def _():
            add_relay(n - 3)

        @pl.when(n >= 6)
        def _():
            add_main(n - 6)

        @pl.when(n < UNITS)
        def _():
            project(n)

        @pl.when((n < UNITS - 2) & (lax.rem(n, 2) == 1))
        def _():
            add_twin(n - 1)
            add_twin(n)

        @pl.when((n >= UNITS - 2) & (n < UNITS))
        def _():
            add_twin(n)

        return carry

    lax.fori_loop(0, UNITS + 6, unit, 0)

    def arrived(n, carry):
        i, r = 1 + lax.div(n, 2), lax.rem(n, 2)
        place = obuf.at[
            pl.ds(pl.multiple_of(r * HALF, HALF), HALF),
            pl.ds(pl.multiple_of(ring(x + x_offset(i), NX) * WIDE, WIDE), WIDE),
        ]
        remote(fbuf.at[0], place, fs.at[0], fr.at[i, r], x_right).wait_recv()
        return carry

    lax.fori_loop(0, UNITS - 2, arrived, 0)
    out_copy = pltpu.make_async_copy(obuf, out, local.at[0])
    out_copy.start()

    for way in (0, 1):
        a_first(0, way).wait_send()
        a_first(1, way).wait_send()
        a_second(0, way).wait_send()
        a_second(1, way).wait_send()

    def sent_unit(u, carry):
        twin_copy(u).wait_send()
        for way in (0, 1):
            relay(u, way).wait_send()
            main(u, way).wait_send()

        @pl.when(u >= 2)
        def _():
            i, r = unit_place(u)
            home(u, i, r).wait_send()

        return carry

    lax.fori_loop(0, UNITS, sent_unit, 0)
    out_copy.wait()


def shards(lengths, queries, keys, values, out_weight):
    bf16, f32 = jnp.bfloat16, jnp.float32
    dma = pltpu.SemaphoreType.DMA
    vmem = pl.BlockSpec(memory_space=pltpu.VMEM)
    any_space = pl.BlockSpec(memory_space=pl.ANY)
    return pl.pallas_call(
        kernel,
        out_shape=jax.ShapeDtypeStruct(queries.shape, bf16),
        in_specs=[
            pl.BlockSpec(memory_space=pltpu.SMEM), any_space, vmem, vmem, any_space
        ],
        out_specs=any_space,
        scratch_shapes=[
            pltpu.VMEM((SLOTS, DEPTH), bf16),
            pltpu.VMEM((NZ, 2, KEYS, HD), bf16),
            pltpu.VMEM((NZ, KEYS, HD), bf16),
            pltpu.VMEM((HEADS, SLOTS, 2 * HD), f32),
            pltpu.VMEM((HEADS, SLOTS, HD), f32),
            pltpu.VMEM((NZ, DEPTH, WIDE), bf16),
            pltpu.VMEM((NX, 2, HALF, DEPTH), bf16),
            pltpu.VMEM((UNITS, NY, HALF, WIDE), bf16),
            pltpu.VMEM((UNITS, NY, HALF, WIDE), bf16),
            pltpu.VMEM((UNITS, NY, HALF, WIDE), f32),
            pltpu.VMEM((UNITS, 2, HALF, HD), bf16),
            pltpu.VMEM((UNITS, 2, HALF, HD), bf16),
            pltpu.VMEM((UNITS, 2, HALF, WIDE), bf16),
            pltpu.VMEM((UNITS, 2, HALF, WIDE), bf16),
            pltpu.VMEM((UNITS, HALF, WIDE), bf16),
            pltpu.VMEM((SLOTS, DEPTH), bf16),
            dma((2,)),
            dma((8,)), dma((9,)),
            dma((2, 8)), dma((2, 8)), dma((2, 8)), dma((2, 8)),
            dma((2, SENDS)), dma((2, SENDS)),
            dma((2, 2)), dma((2, 2)), dma((4, 2)), dma((2, 2)),
            dma((UNITS,)), dma((UNITS,)),
            dma((UNITS, 2)), dma((UNITS, 2)),
            dma((UNITS, 2)), dma((UNITS, 2)),
            dma((UNITS,)), dma((4, 2)),
        ],
        compiler_params=pltpu.CompilerParams(
            collective_id=0, has_side_effects=True, vmem_limit_bytes=56 * 1024 * 1024
        ),
        cost_estimate=pl.CostEstimate(
            flops=16_000_000_000, bytes_accessed=4_000_000, transcendentals=21_000_000
        ),
    )(lengths, queries, keys, values, out_weight)


def solution(mesh):
    return jax.shard_map(
        shards,
        mesh=mesh,
        in_specs=(P(), P("ctx", "tp"), P("ctx", "tp"), P("ctx", "tp"), P("tp", "ctx")),
        out_specs=P("ctx", "tp"),
        check_vma=False,
    )
```
